512 devices in a mesh: dp: 8 (over y, core), seq: 64 (over x, z).
Axes of the slice: x: 4, y: 4, z: 16, core: 2. Of those that a mesh axis runs over, the one named last changes fastest.
Arguments:
- queries: bfloat16 [8, 16384, 384], P('dp', 'seq'), may hold values from -6 to 6
- keys: bfloat16 [8, 16384, 384], P('dp', 'seq'), may hold values from -6 to 6
- values: bfloat16 [8, 16384, 384], P('dp', 'seq'), may hold values from -6 to 6
- outputs: bfloat16 [8, 16384, 384], P('dp', 'seq'), may hold values from -16 to 16
- d_final: bfloat16 [8, 16384, 768], P('dp', 'seq'), may hold values from -6 to 6
- stats: float32 [8, 16384, 8], P('dp', 'seq'), may hold values from 6.5 to 8
- w_out: bfloat16 [384, 768], replicated, may hold values from -0.21875 to 0.21875
Outputs:
- d_queries: bfloat16 [8, 16384, 384], P('dp', 'seq')
- d_keys: bfloat16 [8, 16384, 384], P('dp', 'seq')
- d_values: bfloat16 [8, 16384, 384], P('dp', 'seq')
- grad_weight: float32 [384, 768], P('seq')
The draws below stay inside these ranges and needn't reach their ends.
All inputs are finite; a program needn't handle non-finite values.
Results may differ from the reference program's by a relative error of at most 0.0057.
Values may be sent and summed in bfloat16 or wider, within the bound.
No kernel may reach another device: no remote copies, remote signals or barrier semaphores. Data moves between devices by JAX's collectives and lax.ppermute only.
A program may use at most 64 MiB of HBM per device.

```python
import jax
import jax.numpy as jnp
from jax import lax

HEADS = 8
HD = 48
D = 768
GROUP = 8
TOK_DEV = 256
SLIDES = 8
S = 16384
N_SEQ = 64


def spiked(entries, own_key, source, target, shards_of, factor):
    owner, partner = [(jnp.arange(entries.shape[axis_at]) // (entries.shape[axis_at] // shards_of)).reshape([-1 if axis == axis_at else 1 for axis in range(entries.ndim)]) for axis_at in (source, target)]
    chosen = jax.random.permutation(own_key, shards_of)[partner]
    strong = (owner == chosen) | (owner == (partner + shards_of // 2) % shards_of)
    return jnp.where(strong, factor * entries, entries)


def shard_levels(rng, extent, shards, low, top_value):
    loudness = 1.0
    for dim, blocks in shards:
        steps = jax.random.uniform(jax.random.fold_in(jax.random.fold_in(rng, 6), dim), (blocks,), jnp.float32, low / len(shards), top_value / len(shards))
        loudness = loudness * jnp.repeat(jnp.exp(steps), extent[dim] // blocks).reshape((-1,) + (1,) * (len(extent) - 1 - dim))
    return loudness


def bell_draw(key, shape, scale, reach, shards=(), kind=jnp.bfloat16):
    level = shard_levels(key, shape, shards, -0.22, 0.18) if shards else 1.0
    array = jax.random.normal(key, shape, jnp.float32) * scale * level
    return jnp.minimum(jnp.maximum(array, -reach), reach).astype(kind)


def bell_draw_with(key, extent, scale, limit, split, heavy, kind=jnp.bfloat16):
    array = scale * jax.random.normal(key, extent, jnp.float32)
    if split:
        array = array * shard_levels(key, extent, split, -0.22, 0.18)
    return jnp.clip(spiked(array, jax.random.fold_in(key, 3), *heavy), -limit, limit).astype(kind)


def setup_inputs(seed: int = 0) -> dict:
    key_of = jax.random.split(jax.random.key(seed), 8)
    return {
        "queries": bell_draw(key_of[0], (SLIDES, S, HEADS * HD), 1.0, 6.0, ((0, 8), (1, 64))),
        "keys": bell_draw(key_of[1], (SLIDES, S, HEADS * HD), 1.0, 6.0, ((0, 8), (1, 64))),
        "values": bell_draw(key_of[2], (SLIDES, S, HEADS * HD), 1.0, 6.0, ((0, 8), (1, 64))),
        "outputs": bell_draw_with(key_of[3], (SLIDES, S, HEADS * HD), 1.0, 16.0, ((0, 8), (1, 64)), (1, 2, 64, 4.0)),
        "d_final": bell_draw(key_of[4], (SLIDES, S, D), 1.0, 6.0, ((0, 8), (1, 64))),
        "stats": jnp.clip(6.5 + 1.5 * jax.random.uniform(key_of[5], (SLIDES, S, HEADS), jnp.float32) ** shard_levels(key_of[5], (SLIDES, S, HEADS), ((0, 8), (1, 64)), -0.2, 0.2), 6.5, 8.0),
        "w_out": bell_draw(key_of[6], (HEADS * HD, D), D ** -0.5, 0.21875),
    }


def pick(x, stride, span, heads):
    rows = x.shape[0]
    shaped = x.reshape(rows // span, span // stride, stride, heads, x.shape[-1])
    return jnp.stack([shaped[:, :, h % stride, h, :] for h in range(heads)], axis=2)


def place(y, stride, span, heads, rows):
    shaped = jnp.zeros((rows // span, span // stride, stride, heads, y.shape[-1]), jnp.float32)
    for h in range(heads):
        shaped = shaped.at[:, :, h % stride, h, :].set(y[:, :, h, :])
    return shaped.reshape(rows, heads, y.shape[-1])


def set_backward(query, d_out, lse, delta, keys, values, scale):
    query = query.astype(jnp.float32)
    d_out_f = d_out.astype(jnp.float32)
    keys = keys.astype(jnp.float32)
    values = values.astype(jnp.float32)
    scores = jnp.einsum("nhc,mhc->hnm", query, keys) * scale
    probs = jnp.exp(scores - jnp.transpose(lse)[:, :, None])
    d_probs = jnp.einsum("nhc,mhc->hnm", d_out_f, values)
    d_scores = (probs * (d_probs - jnp.transpose(delta)[:, :, None])).astype(jnp.bfloat16).astype(jnp.float32)
    probs_low = probs.astype(jnp.bfloat16).astype(jnp.float32)
    d_query = jnp.einsum("hnm,mhc->nhc", d_scores, keys) * scale
    d_key = jnp.einsum("hnm,nhc->mhc", d_scores, query) * scale
    d_value = jnp.einsum("hnm,nhc->mhc", probs_low, d_out_f)
    return d_query, d_key, d_value


def reference(queries, keys, values, outputs, d_final, stats, w_out):
    scale = float(HD) ** -0.5
    levels = ((1, TOK_DEV), (GROUP, GROUP * TOK_DEV), (N_SEQ, S))

    def one_slide(items):
        q, k, v, o, dy, lse = items
        d_out = jnp.dot(dy, jnp.transpose(w_out), preferred_element_type=jnp.float32).astype(jnp.bfloat16)
        o3 = o.reshape(S, HEADS, HD)
        d3 = d_out.reshape(S, HEADS, HD)
        delta = jnp.sum(d3.astype(jnp.float32) * o3.astype(jnp.float32), axis=-1)
        grad_w = jnp.dot(jnp.transpose(o), dy, preferred_element_type=jnp.float32)
        q3 = q.reshape(S, HEADS, HD)
        k3 = k.reshape(S, HEADS, HD)
        v3 = v.reshape(S, HEADS, HD)
        total_q = jnp.zeros((S, HEADS, HD), jnp.float32)
        total_k = jnp.zeros((S, HEADS, HD), jnp.float32)
        total_v = jnp.zeros((S, HEADS, HD), jnp.float32)
        for stride, span in levels:
            pq = pick(q3, stride, span, HEADS)
            pk = pick(k3, stride, span, HEADS)
            pv = pick(v3, stride, span, HEADS)
            pd = pick(d3, stride, span, HEADS)
            pl = pick(lse[:, :, None], stride, span, HEADS)[..., 0]
            pdl = pick(delta[:, :, None], stride, span, HEADS)[..., 0]
            dq, dk, dv = lax.map(lambda a: set_backward(a[0], a[1], a[2], a[3], a[4], a[5], scale), (pq, pd, pl, pdl, pk, pv))
            total_q = total_q + place(dq, stride, span, HEADS, S)
            total_k = total_k + place(dk, stride, span, HEADS, S)
            total_v = total_v + place(dv, stride, span, HEADS, S)
        width = HEADS * HD
        return (total_q.reshape(S, width).astype(jnp.bfloat16), total_k.reshape(S, width).astype(jnp.bfloat16), total_v.reshape(S, width).astype(jnp.bfloat16), grad_w)

    dq_all, dk_all, dv_all, grads = lax.map(one_slide, (queries, keys, values, outputs, d_final, stats))
    return (dq_all, dk_all, dv_all, jnp.sum(grads, axis=0))
```

```python
import functools

import jax
import jax.numpy as jnp
from jax import lax
from jax.experimental import pallas as pl
from jax.experimental.pallas import tpu as pltpu
from jax.sharding import PartitionSpec as P

HEADS = 8
HD = 48
GROUP = 8
BF = jnp.bfloat16
F32 = jnp.float32


def iota(shape, dim):
    return lax.broadcasted_iota(jnp.int32, shape, dim)


def dot(a, b, ca, cb):
    return lax.dot_general(a, b, (((ca,), (cb,)), ((), ())), preferred_element_type=F32)


def split(x):
    hi = x.astype(BF)
    return hi, (x - hi.astype(F32)).astype(BF)


def eye(n):
    return (iota((n, n), 0) == iota((n, n), 1)).astype(BF)


def packed_token(p):
    return 64 * (p & 3) + 8 * ((p >> 2) & 7) + (p >> 5)


def spread(part, shape, lane_dim, channel_dim):
    return (iota(shape, lane_dim) == HD * part + lax.rem(iota(shape, channel_dim), HD)).astype(BF)


def own_head(rows, width):
    return lax.div(iota((rows, width), 1), HD) == (iota((rows, width), 0) & (GROUP - 1))


def one_hot(rows, cols, row_of):
    return (iota((rows, cols), 0) == row_of(iota((rows, cols), 1))).astype(BF)


def pre_kernel(q_ref, k_ref, v_ref, o_ref, dy_ref, lse_ref, w_ref, pay_ref, top_ref, do_ref, delta_ref):
    rows, width = q_ref.shape
    d_out = dot(dy_ref[...], w_ref[...], 1, 1).astype(BF)
    do_ref[...] = d_out
    hi, lo = split(d_out.astype(F32) * o_ref[...].astype(F32))
    heads = (lax.div(iota((width, 128), 0), HD) == iota((width, 128), 1)).astype(BF)
    delta = dot(hi, heads, 1, 0) + dot(lo, heads, 1, 0)
    delta_ref[...] = delta[:, :HEADS]
    mine = own_head(rows, width)
    pay = jnp.zeros((rows, 256), F32)
    for part, x in enumerate((q_ref[...], k_ref[...], v_ref[...], d_out)):
        pay += dot(jnp.where(mine, x, jnp.zeros_like(x)), spread(part, (width, 256), 1, 0), 1, 0)
    pick = iota((rows, HEADS), 1) == (iota((rows, HEADS), 0) & (GROUP - 1))
    lane = iota((rows, 256), 1)
    for base, x in ((4 * HD, lse_ref[...]), (4 * HD + 3, delta[:, :HEADS])):
        own = jnp.sum(jnp.where(pick, x, 0.0), axis=1, keepdims=True)
        for n in range(3):
            piece = own.astype(BF).astype(F32)
            pay += jnp.where(lane == base + n, piece, 0.0)
            own = own - piece
    pay = pay.astype(BF)
    perm = (iota((rows, rows), 1) == packed_token(iota((rows, rows), 0))).astype(BF)
    pay_ref[...] = dot(perm, pay, 1, 0).astype(BF)
    at, token = iota((8 * HEADS, rows), 0), iota((8 * HEADS, rows), 1)
    here = token == 64 * (at & 3) + (at >> 3)
    first = (here & ((at & 4) == 0)).astype(BF)
    second = (here & ((at & 4) == 4)).astype(BF)
    top = (dot(first, pay[:, :128], 1, 0) + dot(second, pay[:, 128:], 1, 0)).astype(BF)
    for g in range(top_ref.shape[0]):
        top_ref[g] = top


def weight_kernel(o_ref, dy_ref, gw_ref):
    parts, blocks, block_rows, cols = gw_ref.shape
    o_t = jnp.transpose(o_ref[...])
    for d in range(parts):
        piece = dot(o_t, dy_ref[:, cols * d : cols * (d + 1)], 1, 0).astype(BF)
        for x in range(blocks):
            gw_ref[d, x] = piece[block_rows * x : block_rows * (x + 1)]


def weight_mid_kernel(in_ref, out_ref):
    total = jnp.sum(in_ref[...].astype(F32), axis=0).astype(BF)
    rows, cols = total.shape
    total = jnp.concatenate([total, jnp.zeros((rows, 128 - cols), BF)], axis=1)
    at, row = iota((out_ref.shape[1], rows), 0), iota((out_ref.shape[1], rows), 1)
    each = 8 * rows // out_ref.shape[1]
    sel = (((at & 7) < each) & (row == each * (at >> 3) + (at & 7))).astype(BF)
    spaced = dot(sel, total, 1, 0).astype(BF)
    for d in range(out_ref.shape[0]):
        out_ref[d] = spaced


def weight_end_kernel(in_ref, out_ref):
    each, cols = out_ref.shape
    parts = in_ref.shape[0]
    total = jnp.sum(in_ref[...].astype(F32), axis=1)
    out_ref[...] = jnp.concatenate([total[d, :each, : cols // parts] for d in range(parts)], axis=1)


def window(h):
    lo = HD * h // 128 * 128
    hi = -(-HD * (h + 1) // 128) * 128
    return lo, hi


def padded(x_t, before, total):
    parts = []
    if before:
        parts.append(jnp.zeros((before, x_t.shape[1]), x_t.dtype))
    parts.append(x_t)
    after = total - before - x_t.shape[0]
    if after:
        parts.append(jnp.zeros((after, x_t.shape[1]), x_t.dtype))
    return jnp.concatenate(parts, axis=0)


def set_grads(q_win, do_win, k_pad, v_pad, q_t, k_t, do_t, lse, delta):
    scale = float(HD) ** -0.5
    probs = jnp.exp(dot(q_win, k_pad, 1, 0) * scale - lse)
    d_scores = (probs * (dot(do_win, v_pad, 1, 0) - delta)).astype(BF)
    return (
        dot(k_t, d_scores, 1, 1) * scale,
        dot(q_t, d_scores, 1, 0) * scale,
        dot(do_t, probs.astype(BF), 1, 0),
    )


def local_kernel(q_ref, k_ref, v_ref, do_ref, delta_ref, lse_ref, dq_ref, dk_ref, dv_ref, t_ref):
    q_t, k_t, v_t, do_t = (jnp.transpose(r[...]) for r in (q_ref, k_ref, v_ref, do_ref))
    for h in range(HEADS):
        own = slice(HD * h, HD * (h + 1))
        lo, hi = window(h)
        grads = set_grads(
            q_ref[:, lo:hi],
            do_ref[:, lo:hi],
            padded(k_t[own], HD * h - lo, hi - lo),
            padded(v_t[own], HD * h - lo, hi - lo),
            q_t[own],
            k_t[own],
            do_t[own],
            lse_ref[:, h : h + 1],
            delta_ref[:, h : h + 1],
        )
        for n, g in enumerate(grads):
            t_ref[n, own, :] = g
    for n, out in enumerate((dq_ref, dk_ref, dv_ref)):
        out[...] = jnp.transpose(t_ref[n])


def packed_grads(x):
    x_t = dot(eye(256), x, 1, 1).astype(BF)
    tail = x[:, 128:].astype(F32)

    def column(n):
        at = 4 * HD + 3 * n - 128
        return tail[:, at : at + 1] + tail[:, at + 1 : at + 2] + tail[:, at + 2 : at + 3]

    q_t, k_t, v_t, do_t = (x_t[HD * n : HD * (n + 1)] for n in range(4))
    grads = set_grads(
        x[:, :128], x[:, 128:], padded(k_t, 0, 128), padded(v_t, 3 * HD - 128, 128), q_t, k_t, do_t, column(0), column(1)
    )
    return jnp.concatenate(grads, axis=0)


def group_kernel(x_ref, g_ref):
    g_ref[...] = packed_grads(x_ref[...])


def far_kernel(where_ref, y_ref, g_ref, back_ref):
    at, row = iota((256, 512), 0), iota((256, 512), 1)
    first = (row == 8 * (at >> 2) + (at & 3)).astype(BF)
    second = (row == 8 * (at >> 2) + 4 + (at & 3)).astype(BF)
    y = jnp.concatenate([dot(first, y_ref[...], 1, 0), dot(second, y_ref[...], 1, 0)], axis=1)
    far = packed_grads(y.astype(BF))
    row, col = iota((256, 256), 0), iota((256, 256), 1)
    here = (row >> 5) == where_ref[0]
    sel = (here & (col == 32 * ((row >> 2) & 7) + (row & 3))).astype(BF)
    hi, lo = split(far)
    total = (g_ref[...] + dot(hi, sel, 1, 0) + dot(lo, sel, 1, 0)).astype(BF)
    total = jnp.concatenate([total, jnp.zeros((256 - total.shape[0], 256), BF)], axis=0)
    back_ref[...] = dot(eye(256), total, 1, 1).astype(BF)


def final_kernel(z_ref, dq_ref, dk_ref, dv_ref, oq_ref, ok_ref, ov_ref):
    rows, width = dq_ref.shape
    perm_t = (iota((rows, rows), 0) == packed_token(iota((rows, rows), 1))).astype(BF)
    y = dot(perm_t, z_ref[...], 1, 0).astype(BF)
    mine = own_head(rows, width)
    for n, (near, out) in enumerate(((dq_ref, oq_ref), (dk_ref, ok_ref), (dv_ref, ov_ref))):
        far = dot(y, spread(n, (256, width), 0, 1), 1, 0)
        out[...] = (near[...] + jnp.where(mine, far, 0.0)).astype(BF)


def call(kernel, outs, *args, scratch=(), smem=0, flops=0):
    vmem = pl.BlockSpec(memory_space=pltpu.VMEM)
    return pl.pallas_call(
        kernel,
        out_shape=outs,
        in_specs=[pl.BlockSpec(memory_space=pltpu.SMEM)] * smem + [vmem] * (len(args) - smem),
        out_specs=jax.tree.map(lambda _: vmem, outs),
        scratch_shapes=list(scratch),
        compiler_params=pltpu.CompilerParams(vmem_limit_bytes=32 * 1024 * 1024),
        cost_estimate=pl.CostEstimate(flops=flops, bytes_accessed=2_000_000, transcendentals=0),
    )(*args)


def on_device(queries, keys, values, outputs, d_final, stats, w_out):
    q, k, v, o, dy, lse = (x[0] for x in (queries, keys, values, outputs, d_final, stats))
    rows, width = q.shape
    cols = dy.shape[1]
    dp, blocks, ring = lax.axis_size("dp"), lax.axis_size("x"), lax.axis_size(("zh", "zl"))
    groups = lax.axis_size(("x", "zh"))
    shape = jax.ShapeDtypeStruct

    def exchange(x, axes):
        return lax.all_to_all(x, axes, 0, 0, tiled=True)

    gw = call(
        weight_kernel,
        shape((dp, blocks, width // blocks, cols // dp), BF),
        o, dy,
        flops=150_000_000,
    )
    gw = exchange(gw.reshape(dp * blocks, width // blocks, cols // dp), ("dp", "x"))
    pay, top, d_out, delta = call(
        pre_kernel,
        (
            shape((rows, 256), BF),
            shape((groups, 8 * HEADS, 128), BF),
            shape((rows, width), BF),
            shape((rows, HEADS), F32),
        ),
        q, k, v, o, dy, lse, w_out,
        flops=1_000_000_000,
    )
    tops = exchange(top.reshape(groups * GROUP, 8, 128), ("x", "zh", "zl")).reshape(-1, 128)
    mine = exchange(pay.reshape(GROUP, rows // GROUP, 256), "zl").reshape(256, 256)
    dq0, dk0, dv0 = call(
        local_kernel,
        (shape((rows, width), F32),) * 3,
        q, k, v, d_out, delta, lse,
        scratch=[pltpu.VMEM((3, width, rows), F32)],
        flops=1_000_000_000,
    )
    gw = call(weight_mid_kernel, shape((dp, 8 * ring, 128), BF), gw, flops=10_000_000)
    gw = exchange(gw.reshape(dp * ring, 8, 128), ("dp", "zh", "zl"))
    group = call(group_kernel, shape((3 * HD, 256), F32), mine, flops=100_000_000)
    where = lax.axis_index(("x", "zh")).astype(jnp.int32).reshape(1)
    back = call(far_kernel, shape((256, 256), BF), where, tops, group, smem=1, flops=100_000_000)
    z = exchange(back.reshape(GROUP, rows // GROUP, 256), "zl").reshape(256, 256)
    d_q, d_k, d_v = call(final_kernel, (shape((rows, width), BF),) * 3, z, dq0, dk0, dv0, flops=300_000_000)
    grad_weight = call(
        weight_end_kernel,
        shape((width // (blocks * ring), cols), F32),
        gw.reshape(dp, ring, 8, 128),
        flops=1_000_000,
    )
    return d_q[None], d_k[None], d_v[None], grad_weight


def solution(mesh):
    dp, seq = mesh.devices.shape
    fine = jax.sharding.Mesh(
        mesh.devices.reshape(dp, seq // 16, 16 // GROUP, GROUP), ("dp", "x", "zh", "zl")
    )
    seq_axes = ("x", "zh", "zl")
    placed = P("dp", seq_axes, None)
    return jax.shard_map(
        on_device,
        mesh=fine,
        in_specs=(placed,) * 6 + (P(),),
        out_specs=(placed,) * 3 + (P(seq_axes, None),),
        check_vma=False,
    )
```

```python
import functools

import jax
import jax.numpy as jnp
from jax import lax
from jax.experimental import pallas as pl
from jax.experimental.pallas import tpu as pltpu
from jax.sharding import PartitionSpec as P

HEADS = 8
HD = 48
GROUP = 8
BF = jnp.bfloat16
F32 = jnp.float32


def iota(shape, dim):
    return lax.broadcasted_iota(jnp.int32, shape, dim)


def dot(a, b, ca, cb):
    return lax.dot_general(a, b, (((ca,), (cb,)), ((), ())), preferred_element_type=F32)


def split(x):
    hi = x.astype(BF)
    return hi, (x - hi.astype(F32)).astype(BF)


def eye(n):
    return (iota((n, n), 0) == iota((n, n), 1)).astype(BF)


def packed_token(p):
    return 64 * (p & 3) + 8 * ((p >> 2) & 7) + (p >> 5)


def spread(part, shape, lane_dim, channel_dim):
    return (iota(shape, lane_dim) == HD * part + lax.rem(iota(shape, channel_dim), HD)).astype(BF)


def own_head(rows, width):
    return lax.div(iota((rows, width), 1), HD) == (iota((rows, width), 0) & (GROUP - 1))


def one_hot(rows, cols, row_of):
    return (iota((rows, cols), 0) == row_of(iota((rows, cols), 1))).astype(BF)


def front_kernel(*refs):
    hbm, (pay_ref, out_ref, do_ref, stat_ref), vmem, sems = refs[:7], refs[7:11], refs[11:18], refs[18]
    copies = [pltpu.make_async_copy(a, b, sems.at[n]) for n, (a, b) in enumerate(zip(hbm, vmem))]
    for copy in copies:
        copy.start()
    dy_ref, w_ref, o_ref, lse_ref, q_ref, k_ref, v_ref = vmem
    for copy in copies[:4]:
        copy.wait()
    rows, width = o_ref.shape
    cols = dy_ref.shape[1]
    out, dy = o_ref[...], dy_ref[...]
    d_out = dot(dy, w_ref[...], 1, 1).astype(BF)
    do_ref[...] = d_out
    hi, lo = split(d_out.astype(F32) * out.astype(F32))
    heads = (lax.div(iota((width, 128), 0), HD) == iota((width, 128), 1)).astype(BF)
    delta = (dot(hi, heads, 1, 0) + dot(lo, heads, 1, 0))[:, :HEADS]
    lse = jnp.transpose(lse_ref[...])
    stat_ref[...] = jnp.concatenate([delta, lse], axis=1)
    parts = out_ref.shape[0]
    each = width // parts
    grad = dot(out, dy, 0, 0)
    for x in range(parts):
        for t in range(cols // 128):
            out_ref[x, each * t : each * (t + 1)] = grad[each * x : each * (x + 1), 128 * t : 128 * (t + 1)].astype(BF)
    for copy in copies[4:]:
        copy.wait()
    mine = own_head(rows, width)
    pay = jnp.zeros((rows, 256), F32)
    for part, x in enumerate((q_ref[...], k_ref[...], v_ref[...], d_out)):
        pay += dot(jnp.where(mine, x, jnp.zeros_like(x)), spread(part, (width, 256), 1, 0), 1, 0)
    pick = iota((rows, HEADS), 1) == (iota((rows, HEADS), 0) & (GROUP - 1))
    lane = iota((rows, 256), 1)
    for base, x in ((4 * HD, lse), (4 * HD + 3, delta)):
        own = jnp.sum(jnp.where(pick, x, 0.0), axis=1, keepdims=True)
        for n in range(3):
            piece = own.astype(BF).astype(F32)
            pay += jnp.where(lane == base + n, piece, 0.0)
            own = own - piece
    pay = pay.astype(BF)
    perm = (iota((rows, rows), 1) == packed_token(iota((rows, rows), 0))).astype(BF)
    pay_ref[...] = dot(perm, pay, 1, 0).astype(BF)
    at, token = iota((8 * HEADS, rows), 0), iota((8 * HEADS, rows), 1)
    here = token == 64 * (at & 3) + ((at >> 2) & 7)
    first = (here & (at < 4 * HEADS)).astype(BF)
    second = (here & (at >= 4 * HEADS)).astype(BF)
    top = (dot(first, pay[:, :128], 1, 0) + dot(second, pay[:, 128:], 1, 0)).astype(BF)
    for x in range(parts):
        out_ref[x, width * cols // parts // 128 :] = top


def mid_kernel(in_ref, pay_ref, out_ref):
    parts = in_ref.shape[0]
    ring = out_ref.shape[0]
    count = in_ref.shape[1] - 8 * HEADS
    grad = jnp.sum(in_ref[:, :count].astype(F32), axis=0).astype(BF)
    room = out_ref.shape[1] - 96
    tiles = 6
    each = count // tiles
    few = each // ring
    top = jnp.concatenate([in_ref[x, count:] for x in range(parts)], axis=0)
    n = top.shape[0]
    to, frm = iota((n, n), 0), iota((n, n), 1)
    source = 64 * ((to >> 2) & 3) + 32 * ((to >> 4) & 1) + 4 * (to >> 5) + (to & 3)
    top = dot((frm == source).astype(BF), top, 1, 0).astype(BF)
    big, row = iota((room * ring, count), 0), iota((room * ring, count), 1)
    z, at = lax.div(big[:, :1], room), lax.rem(big[:, :1], room)
    source = jnp.where(at < tiles * few, each * lax.div(at, few) + few * z + lax.rem(at, few), -1)
    grad = dot((row == source).astype(BF), grad, 1, 0).astype(BF)
    for z in range(ring):
        r = z & (GROUP - 1)
        out_ref[z, :32] = pay_ref[32 * r : 32 * (r + 1), :128]
        out_ref[z, 32:64] = pay_ref[32 * r : 32 * (r + 1), 128:]
        out_ref[z, 64:96] = top[32 * r : 32 * (r + 1)]
        out_ref[z, 96:] = grad[room * z : room * (z + 1)]


def weight_kernel(in_ref, _, out_ref):
    each, cols = out_ref.shape
    total = jnp.sum(in_ref[:, 96:].astype(F32), axis=0)
    out_ref[...] = jnp.concatenate([total[each * t : each * (t + 1)] for t in range(cols // 128)], axis=1)


def window(h):
    lo = HD * h // 128 * 128
    hi = -(-HD * (h + 1) // 128) * 128
    return lo, hi


def padded(x_t, before, total):
    parts = []
    if before:
        parts.append(jnp.zeros((before, x_t.shape[1]), x_t.dtype))
    parts.append(x_t)
    after = total - before - x_t.shape[0]
    if after:
        parts.append(jnp.zeros((after, x_t.shape[1]), x_t.dtype))
    return jnp.concatenate(parts, axis=0)


def set_grads(q_win, do_win, k_pad, v_pad, q_t, k_t, do_t, lse, delta):
    scale = float(HD) ** -0.5
    probs = jnp.exp(dot(q_win, k_pad, 1, 0) * scale - lse)
    d_scores = (probs * (dot(do_win, v_pad, 1, 0) - delta)).astype(BF)
    return (
        dot(k_t, d_scores, 1, 1) * scale,
        dot(q_t, d_scores, 1, 0) * scale,
        dot(do_t, probs.astype(BF), 1, 0),
    )


def local_kernel(q_ref, k_ref, v_ref, do_ref, stat_ref, dq_ref, dk_ref, dv_ref, t_ref):
    q_t, k_t, v_t, do_t = (jnp.transpose(r[...]) for r in (q_ref, k_ref, v_ref, do_ref))
    for h in range(HEADS):
        own = slice(HD * h, HD * (h + 1))
        lo, hi = window(h)
        grads = set_grads(
            q_ref[:, lo:hi],
            do_ref[:, lo:hi],
            padded(k_t[own], HD * h - lo, hi - lo),
            padded(v_t[own], HD * h - lo, hi - lo),
            q_t[own],
            k_t[own],
            do_t[own],
            stat_ref[:, HEADS + h : HEADS + h + 1],
            stat_ref[:, h : h + 1],
        )
        for n, g in enumerate(grads):
            t_ref[n, own, :] = g
    for n, out in enumerate((dq_ref, dk_ref, dv_ref)):
        out[...] = jnp.transpose(t_ref[n])


def packed_grads(x):
    x_t = dot(eye(256), x, 1, 1).astype(BF)
    tail = x[:, 128:].astype(F32)

    def column(n):
        at = 4 * HD + 3 * n - 128
        return tail[:, at : at + 1] + tail[:, at + 1 : at + 2] + tail[:, at + 2 : at + 3]

    q_t, k_t, v_t, do_t = (x_t[HD * n : HD * (n + 1)] for n in range(4))
    grads = set_grads(
        x[:, :128], x[:, 128:], padded(k_t, 0, 128), padded(v_t, 3 * HD - 128, 128), q_t, k_t, do_t, column(0), column(1)
    )
    return jnp.concatenate(grads, axis=0)


def joined(in_ref, where, first, count):
    lo = in_ref[where, first : first + count].reshape(256, 128)
    hi = in_ref[where, first + count : first + 2 * count].reshape(256, 128)
    return jnp.concatenate([lo, hi], axis=1)


def group_kernel(where_ref, in_ref, _, g_ref):
    g_ref[...] = packed_grads(joined(in_ref, pl.ds(GROUP * where_ref[1], GROUP), 0, 32))


def far_kernel(where_ref, in_ref, g_ref, back_ref):
    far = packed_grads(joined(in_ref, slice(None), 64, 16))
    row, col = iota((256, 256), 0), iota((256, 256), 1)
    here = ((row >> 7) == where_ref[1]) & (((row >> 2) & 3) == where_ref[0])
    sel = (here & (col == 32 * ((row >> 4) & 7) + (row & 3))).astype(BF)
    hi, lo = split(far)
    total = (g_ref[...] + dot(hi, sel, 1, 0) + dot(lo, sel, 1, 0)).astype(BF)
    total = jnp.concatenate([total, jnp.zeros((256 - total.shape[0], 256), BF)], axis=0)
    back_ref[...] = dot(eye(256), total, 1, 1).astype(BF)


def final_kernel(z_ref, dq_ref, dk_ref, dv_ref, oq_ref, ok_ref, ov_ref):
    rows, width = dq_ref.shape
    perm_t = (iota((rows, rows), 0) == packed_token(iota((rows, rows), 1))).astype(BF)
    y = dot(perm_t, z_ref[...], 1, 0).astype(BF)
    mine = own_head(rows, width)
    for n, (near, out) in enumerate(((dq_ref, oq_ref), (dk_ref, ok_ref), (dv_ref, ov_ref))):
        far = dot(y, spread(n, (256, width), 0, 1), 1, 0)
        out[...] = (near[...] + jnp.where(mine, far, 0.0)).astype(BF)


def call(kernel, outs, *args, scratch=(), smem=0, hbm=False, flops=0):
    vmem = pl.BlockSpec(memory_space=pltpu.VMEM)
    held = pl.BlockSpec(memory_space=pltpu.HBM) if hbm else vmem
    return pl.pallas_call(
        kernel,
        out_shape=outs,
        in_specs=[pl.BlockSpec(memory_space=pltpu.SMEM)] * smem + [held] * (len(args) - smem),
        out_specs=jax.tree.map(lambda _: vmem, outs),
        scratch_shapes=list(scratch),
        compiler_params=pltpu.CompilerParams(vmem_limit_bytes=32 * 1024 * 1024),
        cost_estimate=pl.CostEstimate(flops=flops, bytes_accessed=2_000_000, transcendentals=0),
    )(*args)


def on_device(queries, keys, values, outputs, d_final, stats, w_out):
    q, k, v, o, dy, lse = (x[0] for x in (queries, keys, values, outputs, d_final, stats))
    rows, width = q.shape
    cols = dy.shape[1]
    blocks, ring = lax.axis_size("x"), lax.axis_size(("zh", "zl"))
    shape = jax.ShapeDtypeStruct

    def exchange(x, axes):
        return lax.all_to_all(x, axes, 0, 0, tiled=True)

    ins = (dy, w_out, o, lse.T, q, k, v)
    pay, out, d_out, stat = call(
        front_kernel,
        (
            shape((rows, 256), BF),
            shape((blocks, width * cols // blocks // 128 + 8 * HEADS, 128), BF),
            shape((rows, width), BF),
            shape((rows, 2 * HEADS), F32),
        ),
        *ins,
        hbm=True,
        scratch=[pltpu.VMEM(x.shape, x.dtype) for x in ins] + [pltpu.SemaphoreType.DMA((len(ins),))],
        flops=1_000_000_000,
    )
    over_x = exchange(out, "x")
    out = call(mid_kernel, shape((ring, 144, 128), BF), over_x, pay, flops=100_000_000)
    over_z = exchange(out, ("zh", "zl"))
    near = call(
        local_kernel,
        (shape((rows, width), F32),) * 3,
        q, k, v, d_out, stat,
        scratch=[pltpu.VMEM((3, width, rows), F32)],
        flops=1_000_000_000,
    )
    where = jnp.stack([lax.axis_index("x"), lax.axis_index("zh")]).astype(jnp.int32)
    group = call(group_kernel, shape((3 * HD, 256), F32), where, over_z, near[0], smem=1, flops=100_000_000)
    back = call(far_kernel, shape((256, 256), BF), where, over_z, group, smem=1, flops=100_000_000)
    z = exchange(back.reshape(GROUP, rows // GROUP, 256), "zl").reshape(256, 256)
    grad = call(weight_kernel, shape((width // (blocks * ring), cols), F32), over_z, near[0], flops=1_000_000)
    members = lax.axis_size("dp")
    for bit in range(members.bit_length() - 1):
        grad = grad + lax.ppermute(grad, "dp", [(i, i ^ (1 << bit)) for i in range(members)])
    d_q, d_k, d_v = call(final_kernel, (shape((rows, width), BF),) * 3, z, *near, flops=300_000_000)
    return d_q[None], d_k[None], d_v[None], grad


def solution(mesh):
    dp, seq = mesh.devices.shape
    fine = jax.sharding.Mesh(
        mesh.devices.reshape(dp, seq // 16, 16 // GROUP, GROUP), ("dp", "x", "zh", "zl")
    )
    seq_axes = ("x", "zh", "zl")
    placed = P("dp", seq_axes, None)
    return jax.shard_map(
        on_device,
        mesh=fine,
        in_specs=(placed,) * 6 + (P(),),
        out_specs=(placed,) * 3 + (P(seq_axes, None),),
        check_vma=False,
    )
```

```python
import functools

import jax
import jax.numpy as jnp
from jax import lax
from jax.experimental import pallas as pl
from jax.experimental.pallas import tpu as pltpu
from jax.sharding import PartitionSpec as P

HEADS = 8
HD = 48
GROUP = 8
CORES = 2
ROOM = 60
BF = jnp.bfloat16
F32 = jnp.float32


def iota(shape, dim):
    return lax.broadcasted_iota(jnp.int32, shape, dim)


def dot(a, b, ca, cb):
    return lax.dot_general(a, b, (((ca,), (cb,)), ((), ())), preferred_element_type=F32)


def split(x):
    hi = x.astype(BF)
    return hi, (x - hi.astype(F32)).astype(BF)


def eye(n):
    return (iota((n, n), 0) == iota((n, n), 1)).astype(BF)


def packed_token(p):
    return 64 * (p & 3) + 8 * ((p >> 2) & 7) + (p >> 5)


def spread(part, shape, lane_dim, channel_dim):
    return (iota(shape, lane_dim) == HD * part + lax.rem(iota(shape, channel_dim), HD)).astype(BF)


def own_head(rows, width):
    return lax.div(iota((rows, width), 1), HD) == (iota((rows, width), 0) & (GROUP - 1))


def one_hot(rows, cols, row_of):
    return (iota((rows, cols), 0) == row_of(iota((rows, cols), 1))).astype(BF)


def front_kernel(*refs):
    hbm, (pay_ref, out_ref, do_ref, stat_ref), vmem, sems = refs[:7], refs[7:11], refs[11:18], refs[18]
    copies = [pltpu.make_async_copy(a, b, sems.at[n]) for n, (a, b) in enumerate(zip(hbm, vmem))]
    for copy in copies:
        copy.start()
    dy_ref, w_ref, o_ref, lse_ref, q_ref, k_ref, v_ref = vmem
    for copy in copies[:4]:
        copy.wait()
    rows, width = o_ref.shape
    cols = dy_ref.shape[1]
    out, dy = o_ref[...], dy_ref[...]
    d_out = dot(dy, w_ref[...], 1, 1).astype(BF)
    do_ref[...] = d_out
    hi, lo = split(d_out.astype(F32) * out.astype(F32))
    heads = (lax.div(iota((width, 128), 0), HD) == iota((width, 128), 1)).astype(BF)
    delta = (dot(hi, heads, 1, 0) + dot(lo, heads, 1, 0))[:, :HEADS]
    lse = jnp.transpose(lse_ref[...])
    stat_ref[...] = jnp.concatenate([delta, lse], axis=1)
    parts = out_ref.shape[0]
    each, half = width * CORES // parts, cols // CORES
    grad = dot(out, dy, 0, 0)
    for n in range(parts):
        x, c = divmod(n, CORES)
        for t in range(half // 128):
            tile = grad[each * x : each * (x + 1), half * c + 128 * t : half * c + 128 * (t + 1)]
            out_ref[n, each * t : each * (t + 1)] = tile.astype(BF)
    for copy in copies[4:]:
        copy.wait()
    mine = own_head(rows, width)
    pay = jnp.zeros((rows, 256), F32)
    for part, x in enumerate((q_ref[...], k_ref[...], v_ref[...], d_out)):
        pay += dot(jnp.where(mine, x, jnp.zeros_like(x)), spread(part, (width, 256), 1, 0), 1, 0)
    pick = iota((rows, HEADS), 1) == (iota((rows, HEADS), 0) & (GROUP - 1))
    lane = iota((rows, 256), 1)
    for base, x in ((4 * HD, lse), (4 * HD + 3, delta)):
        own = jnp.sum(jnp.where(pick, x, 0.0), axis=1, keepdims=True)
        for n in range(3):
            piece = own.astype(BF).astype(F32)
            pay += jnp.where(lane == base + n, piece, 0.0)
            own = own - piece
    pay = pay.astype(BF)
    perm = (iota((rows, rows), 1) == packed_token(iota((rows, rows), 0))).astype(BF)
    pay_ref[...] = dot(perm, pay, 1, 0).astype(BF)
    at, token = iota((8 * HEADS, rows), 0), iota((8 * HEADS, rows), 1)
    here = token == 64 * (at & 3) + ((at >> 2) & 7)
    first = (here & (at < 4 * HEADS)).astype(BF)
    second = (here & (at >= 4 * HEADS)).astype(BF)
    top = (dot(first, pay[:, :128], 1, 0) + dot(second, pay[:, 128:], 1, 0)).astype(BF)
    for n in range(parts):
        out_ref[n, width * cols // parts // 128 :] = top


def mid_kernel(where_ref, in_ref, pay_ref, out_ref):
    ring = out_ref.shape[0]
    count = in_ref.shape[1] - 8 * HEADS
    sums = jnp.sum(in_ref[:, :count].astype(F32), axis=0)
    each = count // 3
    few = each // ring
    wide = jnp.concatenate([sums[each * t : each * (t + 1)] for t in range(3)], axis=1)
    chunks = jnp.concatenate([wide[:, HD * u : HD * (u + 1)] for u in range(8)], axis=0).astype(BF)
    n = chunks.shape[0]
    to = iota((n, 1), 0)
    third, z, p = to >> 8, (to >> 4) & 15, to & 15
    q = 16 * third + p
    source = each * (q & 7) + few * z + (q >> 3)
    grad = dot((iota((n, n), 1) == source).astype(BF), chunks, 1, 0)
    grad = jnp.concatenate([grad[256 * t : 256 * (t + 1)] for t in range(3)], axis=1)
    top = jnp.concatenate([in_ref[CORES * x + where_ref[2], count:] for x in range(4)], axis=0)
    n = top.shape[0]
    to = iota((n, 1), 0)
    source = 64 * ((to >> 2) & 3) + 32 * ((to >> 4) & 1) + 4 * (to >> 5) + (to & 3)
    top = dot((iota((n, n), 1) == source).astype(BF), top, 1, 0)
    for z in range(ring):
        r = z & (GROUP - 1)
        out_ref[z, :32] = pay_ref[32 * r : 32 * (r + 1), :128]
        rest = pay_ref[32 * r : 32 * (r + 1), 128:].astype(F32)
        out_ref[z, 32:48] = jnp.concatenate([rest[:16, :64], rest[16:, :64]], axis=1).astype(BF)
        out_ref[z, 48:64] = top[32 * r : 32 * r + 16].astype(BF)
        mixed = [
            top[32 * r + 16 : 32 * (r + 1), :72],
            rest[:16, 64:72],
            rest[16:, 64:72],
            jnp.zeros((16, 24), F32),
            grad[16 * z : 16 * (z + 1), 128:],
        ]
        out_ref[z, 64:80] = jnp.concatenate(mixed, axis=1).astype(BF)
        out_ref[z, 80:] = grad[16 * z : 16 * (z + 1), :128].astype(BF)


def weight_kernel(in_ref, _, out_ref):
    main = jnp.sum(in_ref[:, 80:].astype(F32), axis=0)
    tail = jnp.sum(in_ref[:, 64:80].astype(F32), axis=0)
    out_ref[...] = jnp.concatenate([main, tail], axis=1)


def weight_end_kernel(in_ref, out_ref):
    each = out_ref.shape[0]
    parts = []
    for c in range(CORES):
        total = in_ref[c]
        for y in range(1, in_ref.shape[0] // CORES):
            total = total + in_ref[CORES * y + c]
        total = jnp.concatenate([total[:, :128], total[:, 240:]], axis=1)
        chunks = jnp.concatenate([total[:, HD * t : HD * (t + 1)] for t in range(3)], axis=0).reshape(each, 8, HD)
        parts += [chunks[:, u, :] for u in range(8)]
    out_ref[...] = jnp.concatenate(parts, axis=1)


def window(h):
    lo = HD * h // 128 * 128
    hi = -(-HD * (h + 1) // 128) * 128
    return lo, hi


def padded(x_t, before, total):
    parts = []
    if before:
        parts.append(jnp.zeros((before, x_t.shape[1]), x_t.dtype))
    parts.append(x_t)
    after = total - before - x_t.shape[0]
    if after:
        parts.append(jnp.zeros((after, x_t.shape[1]), x_t.dtype))
    return jnp.concatenate(parts, axis=0)


def set_grads(q_win, do_win, k_pad, v_pad, q_t, k_t, do_t, lse, delta):
    scale = float(HD) ** -0.5
    probs = jnp.exp(dot(q_win, k_pad, 1, 0) * scale - lse)
    d_scores = (probs * (dot(do_win, v_pad, 1, 0) - delta)).astype(BF)
    return (
        dot(k_t, d_scores, 1, 1) * scale,
        dot(q_t, d_scores, 1, 0) * scale,
        dot(do_t, probs.astype(BF), 1, 0),
    )


def local_kernel(q_ref, k_ref, v_ref, do_ref, stat_ref, dq_ref, dk_ref, dv_ref, t_ref):
    q_t, k_t, v_t, do_t = (jnp.transpose(r[...]) for r in (q_ref, k_ref, v_ref, do_ref))
    for h in range(HEADS):
        own = slice(HD * h, HD * (h + 1))
        lo, hi = window(h)
        grads = set_grads(
            q_ref[:, lo:hi],
            do_ref[:, lo:hi],
            padded(k_t[own], HD * h - lo, hi - lo),
            padded(v_t[own], HD * h - lo, hi - lo),
            q_t[own],
            k_t[own],
            do_t[own],
            stat_ref[:, HEADS + h : HEADS + h + 1],
            stat_ref[:, h : h + 1],
        )
        for n, g in enumerate(grads):
            t_ref[n, own, :] = g
    for n, out in enumerate((dq_ref, dk_ref, dv_ref)):
        out[...] = jnp.transpose(t_ref[n])


def packed_grads(lo, hi, stat):
    x = jnp.concatenate([lo.astype(F32), hi, jnp.zeros_like(hi)], axis=1).astype(BF)
    x_t = dot(eye(256), x, 1, 1).astype(BF)
    q_t, k_t, v_t, do_t = (x_t[HD * n : HD * (n + 1)] for n in range(4))
    lse, delta = (stat[:, n : n + 1] + stat[:, n + 1 : n + 2] + stat[:, n + 2 : n + 3] for n in (0, 3))
    grads = set_grads(
        x[:, :128], x[:, 128:], padded(k_t, 0, 128), padded(v_t, 3 * HD - 128, 128), q_t, k_t, do_t, lse, delta
    )
    return jnp.concatenate(grads, axis=0)


def sets_kernel(where_ref, in_ref, _, back_ref):
    own = pl.ds(GROUP * where_ref[1], GROUP)
    pairs = in_ref[own, 32:48].astype(F32)
    mixed = in_ref[:, 64:80].astype(F32)
    mine = in_ref[own, 64:80].astype(F32)
    group = packed_grads(
        in_ref[own, :32].reshape(256, 128),
        jnp.concatenate([pairs[:, :, :64], pairs[:, :, 64:]], axis=1).reshape(256, 64),
        jnp.concatenate([mine[:, :, 72:80], mine[:, :, 80:88]], axis=1).reshape(256, 8),
    )
    mixed = mixed.reshape(256, 128)
    far = packed_grads(in_ref[:, 48:64].reshape(256, 128), mixed[:, :64], mixed[:, 64:72])
    row, col = iota((256, 256), 0), iota((256, 256), 1)
    here = ((row >> 7) == where_ref[1]) & (((row >> 2) & 3) == where_ref[0])
    sel = (here & (col == 32 * ((row >> 4) & 7) + (row & 3))).astype(BF)
    hi, lo = split(far)
    total = (group + dot(hi, sel, 1, 0) + dot(lo, sel, 1, 0)).astype(BF)
    total = jnp.concatenate([total, jnp.zeros((256 - total.shape[0], 256), BF)], axis=0)
    total = dot(eye(256), total, 1, 1)
    for src in range(GROUP):
        rows = total[32 * src : 32 * (src + 1)]
        back_ref[src, :32] = rows[:, :128].astype(BF)
        tail = [rows[:16, 128:144], rows[16:, 128:144], jnp.zeros((16, 96), F32)]
        back_ref[src, 32:] = jnp.concatenate(tail, axis=1).astype(BF)


def final_kernel(z_ref, dq_ref, dk_ref, dv_ref, oq_ref, ok_ref, ov_ref):
    rows, width = dq_ref.shape
    perm_t = (iota((rows, rows), 0) == packed_token(iota((rows, rows), 1))).astype(BF)
    tail = z_ref[:, 32:].astype(F32)
    tail = jnp.concatenate([tail[:, :, :16], tail[:, :, 16:32]], axis=1).reshape(rows, 16)
    lanes = [z_ref[:, :32].reshape(rows, 128).astype(F32), tail, jnp.zeros((rows, 112), F32)]
    y = dot(perm_t, jnp.concatenate(lanes, axis=1).astype(BF), 1, 0).astype(BF)
    mine = own_head(rows, width)
    for n, (near, out) in enumerate(((dq_ref, oq_ref), (dk_ref, ok_ref), (dv_ref, ov_ref))):
        far = dot(y, spread(n, (256, width), 0, 1), 1, 0)
        out[...] = (near[...] + jnp.where(mine, far, 0.0)).astype(BF)


def call(kernel, outs, *args, scratch=(), smem=0, hbm=False, flops=0, room=32):
    vmem = pl.BlockSpec(memory_space=pltpu.VMEM)
    held = pl.BlockSpec(memory_space=pltpu.HBM) if hbm else vmem
    return pl.pallas_call(
        kernel,
        out_shape=outs,
        in_specs=[pl.BlockSpec(memory_space=pltpu.SMEM)] * smem + [held] * (len(args) - smem),
        out_specs=jax.tree.map(lambda _: vmem, outs),
        scratch_shapes=list(scratch),
        compiler_params=pltpu.CompilerParams(vmem_limit_bytes=room * 1024 * 1024),
        cost_estimate=pl.CostEstimate(flops=flops, bytes_accessed=2_000_000, transcendentals=0),
    )(*args)


def on_device(queries, keys, values, outputs, d_final, stats, w_out):
    q, k, v, o, dy, lse = (x[0] for x in (queries, keys, values, outputs, d_final, stats))
    rows, width = q.shape
    cols = dy.shape[1]
    blocks, ring = lax.axis_size("x"), lax.axis_size(("zh", "zl"))
    shape = jax.ShapeDtypeStruct

    def exchange(x, axes):
        return lax.all_to_all(x, axes, 0, 0, tiled=True)

    ins = (dy, w_out, o, lse.T, q, k, v)
    parts = blocks * CORES
    pay, out, d_out, stat = call(
        front_kernel,
        (
            shape((rows, 256), BF),
            shape((parts, width * cols // parts // 128 + 8 * HEADS, 128), BF),
            shape((rows, width), BF),
            shape((rows, 2 * HEADS), F32),
        ),
        *ins,
        hbm=True,
        room=ROOM,
        scratch=[pltpu.VMEM(x.shape, x.dtype) for x in ins] + [pltpu.SemaphoreType.DMA((len(ins),))],
        flops=1_000_000_000,
    )
    where = jnp.stack([lax.axis_index(a) for a in ("x", "zh", "c")]).astype(jnp.int32)
    over_x = exchange(out, ("x", "c"))
    out = call(mid_kernel, shape((ring, 96, 128), BF), where, over_x, pay, smem=1, flops=100_000_000)
    over_z = exchange(out, ("zh", "zl"))
    near = call(
        local_kernel,
        (shape((rows, width), F32),) * 3,
        q, k, v, d_out, stat,
        scratch=[pltpu.VMEM((3, width, rows), F32)],
        flops=1_000_000_000,
    )
    back = call(sets_kernel, shape((GROUP, 48, 128), BF), where, over_z, near[0], smem=1, flops=200_000_000)
    z = exchange(back, "zl")
    grad = call(weight_kernel, shape((16, 256), F32), over_z, near[0], flops=1_000_000)
    grad = lax.all_gather(grad, ("y", "c"), axis=0)
    grad = call(weight_end_kernel, shape((width // (blocks * ring), cols), F32), grad, flops=1_000_000)
    d_q, d_k, d_v = call(final_kernel, (shape((rows, width), BF),) * 3, z, *near, flops=300_000_000)
    return d_q[None], d_k[None], d_v[None], grad


def solution(mesh):
    dp, seq = mesh.devices.shape
    fine = jax.sharding.Mesh(
        mesh.devices.reshape(dp // CORES, CORES, seq // 16, 16 // GROUP, GROUP), ("y", "c", "x", "zh", "zl")
    )
    dp_axes, seq_axes = ("y", "c"), ("x", "zh", "zl")
    placed = P(dp_axes, seq_axes, None)
    return jax.shard_map(
        on_device,
        mesh=fine,
        in_specs=(placed,) * 6 + (P(),),
        out_specs=(placed,) * 3 + (P(seq_axes, None),),
        check_vma=False,
    )
```

```python
import functools

import jax
import jax.numpy as jnp
from jax import lax
from jax.experimental import pallas as pl
from jax.experimental.pallas import tpu as pltpu
from jax.sharding import PartitionSpec as P

HEADS = 8
HD = 48
GROUP = 8
CORES = 2
ROOM = 60
BF = jnp.bfloat16
F32 = jnp.float32


def iota(shape, dim):
    return lax.broadcasted_iota(jnp.int32, shape, dim)


def dot(a, b, ca, cb):
    return lax.dot_general(a, b, (((ca,), (cb,)), ((), ())), preferred_element_type=F32)


def split(x):
    hi = x.astype(BF)
    return hi, (x - hi.astype(F32)).astype(BF)


def eye(n):
    return (iota((n, n), 0) == iota((n, n), 1)).astype(BF)


def packed_token(p):
    return 64 * (p & 3) + 8 * ((p >> 2) & 7) + (p >> 5)


def spread(part, lanes, width):
    return (iota((1, lanes), 1) - HD * part == lax.rem(iota((width, 1), 0), HD)).astype(BF)


def own_head(rows, width):
    return lax.div(iota((1, width), 1), HD) == (iota((rows, 1), 0) & (GROUP - 1))


def selector(source, count):
    return (iota((source.shape[0], count), 1) == source).astype(BF)


def front_kernel(*refs):
    hbm, outs, vmem, held, (stat_ref, sems) = refs[:7], refs[7:10], refs[11:18], refs[18:21], (refs[10], refs[21])
    copies = [pltpu.make_async_copy(a, b, sems.at[n]) for n, (a, b) in enumerate(zip(hbm, vmem))]
    for copy in copies:
        copy.start()
    dy_ref, o_ref, w_ref, lse_ref, q_ref, k_ref, v_ref = vmem
    out_ref, do_ref, pay_ref = held
    rows, width = o_ref.shape
    cols = dy_ref.shape[1]
    parts = out_ref.shape[0]
    count = width * cols // parts // 128
    leave = [
        pltpu.make_async_copy(held[0].at[:, :count], outs[0].at[:, :count], sems.at[7]),
        pltpu.make_async_copy(held[1], outs[1], sems.at[8]),
        pltpu.make_async_copy(held[2], outs[2], sems.at[9]),
        pltpu.make_async_copy(held[0].at[:, count:], outs[0].at[:, count:], sems.at[10]),
    ]
    copies[0].wait()
    copies[1].wait()
    out, dy = o_ref[...], dy_ref[...]
    each, half = width * CORES // parts, cols // CORES
    grad = dot(out, dy, 0, 0)
    for n in range(parts):
        x, c = divmod(n, CORES)
        for t in range(half // 128):
            tile = grad[each * x : each * (x + 1), half * c + 128 * t : half * c + 128 * (t + 1)]
            out_ref[n, each * t : each * (t + 1)] = tile.astype(BF)
    leave[0].start()
    copies[2].wait()
    copies[3].wait()
    d_out = dot(dy, w_ref[...], 1, 1).astype(BF)
    do_ref[...] = d_out
    leave[1].start()
    hi, lo = split(d_out.astype(F32) * out.astype(F32))
    heads = (lax.div(iota((width, 1), 0), HD) == iota((width, 128), 1)).astype(BF)
    delta = (dot(hi, heads, 1, 0) + dot(lo, heads, 1, 0))[:, :HEADS]
    lse = jnp.transpose(lse_ref[...])
    stat_ref[...] = jnp.concatenate([delta, lse], axis=1)
    for copy in copies[4:]:
        copy.wait()
    mine = own_head(rows, width)
    pay = jnp.zeros((rows, 256), F32)
    for part, x in enumerate((q_ref[...], k_ref[...], v_ref[...], d_out)):
        pay += dot(jnp.where(mine, x, jnp.zeros_like(x)), spread(part, 256, width), 1, 0)
    pick = iota((1, HEADS), 1) == (iota((rows, 1), 0) & (GROUP - 1))
    lane = iota((rows, 128), 1)
    tail = pay[:, 128:]
    for base, x in ((64, lse), (67, delta)):
        own = jnp.sum(jnp.where(pick, x, 0.0), axis=1, keepdims=True)
        for n in range(3):
            piece = own.astype(BF).astype(F32)
            tail += jnp.where(lane == base + n, piece, 0.0)
            own = own - piece
    pay = jnp.concatenate([pay[:, :128], tail], axis=1).astype(BF)
    pay_ref[...] = dot(selector(packed_token(iota((rows, 1), 0)), rows), pay, 1, 0).astype(BF)
    leave[2].start()
    at = iota((8 * HEADS, 1), 0)
    token = 64 * (at & 3) + ((at >> 2) & 7)
    first = selector(jnp.where(at < 4 * HEADS, token, -1), rows)
    second = selector(jnp.where(at < 4 * HEADS, -1, token), rows)
    top = (dot(first, pay[:, :128], 1, 0) + dot(second, pay[:, 128:], 1, 0)).astype(BF)
    for n in range(parts):
        out_ref[n, count:] = top
    leave[3].start()
    for copy in leave:
        copy.wait()


def mid_kernel(where_ref, in_ref, pay_ref, out_ref):
    ring = out_ref.shape[0]
    count = in_ref.shape[1] - 8 * HEADS
    sums = jnp.sum(in_ref[:, :count].astype(F32), axis=0).astype(BF)
    each = count // 3
    few = each // ring
    to = iota((16 * ring, 1), 0)
    z, q = to >> 4, to & 15
    t = (q * 43) >> 8
    main = dot(selector(each * t + few * z + q - few * t, count), sums, 1, 0).astype(BF)
    last = selector(jnp.where(q < 8, 2 * each + few * z + 4 + (q & 1), -1), count)
    last = dot(last, sums, 1, 0)
    lane = iota((1, 128), 1)
    last = jnp.where((lane >> 5) == (q >> 1), last, 0.0).astype(BF)
    last = dot(last, selector(96 + (iota((128, 1), 0) & 31), 128), 1, 0)
    top = jnp.concatenate([in_ref[CORES * x + where_ref[2], count:] for x in range(4)], axis=0)
    to = iota((top.shape[0], 1), 0)
    source = 64 * ((to >> 2) & 3) + 32 * ((to >> 4) & 1) + 4 * (to >> 5) + (to & 3)
    top = dot(selector(source, top.shape[0]), top, 1, 0)
    for r in range(GROUP):
        low = pay_ref[32 * r : 32 * (r + 1), :128]
        rest = pay_ref[32 * r : 32 * (r + 1), 128:].astype(F32)
        pairs = jnp.concatenate([rest[:16, :64], rest[16:, :64]], axis=1).astype(BF)
        near = top[32 * r : 32 * r + 16].astype(BF)
        mixed = [top[32 * r + 16 : 32 * (r + 1), :72], rest[:16, 64:72], rest[16:, 64:72], jnp.zeros((16, 40), F32)]
        mixed = jnp.concatenate(mixed, axis=1)
        for z in range(r, ring, GROUP):
            out_ref[z, :32] = low
            out_ref[z, 32:48] = pairs
            out_ref[z, 48:64] = near
            out_ref[z, 64:80] = (mixed + last[16 * z : 16 * (z + 1)]).astype(BF)
            out_ref[z, 80:] = main[16 * z : 16 * (z + 1)]


def weight_kernel(in_ref, _, out_ref):
    out_ref[:16] = jnp.sum(in_ref[:, 80:].astype(F32), axis=0)
    out_ref[16:] = jnp.sum(in_ref[:, 64:80].astype(F32), axis=0)[:8]


def weight_end_kernel(in_ref, out_ref):
    each = out_ref.shape[0]
    parts = []
    for c in range(CORES):
        total = in_ref[c]
        for y in range(1, in_ref.shape[0] // CORES):
            total = total + in_ref[CORES * y + c]
        last = jnp.concatenate([total[16 + 2 * k : 18 + 2 * k, 96:] for k in range(4)], axis=1)
        total = jnp.concatenate([total[:16], last], axis=0)
        parts += [total[each * t : each * (t + 1)] for t in range(3)]
    out_ref[...] = jnp.concatenate(parts, axis=1)


def window(h):
    lo = HD * h // 128 * 128
    hi = -(-HD * (h + 1) // 128) * 128
    return lo, hi


def padded(x_t, before, total):
    parts = []
    if before:
        parts.append(jnp.zeros((before, x_t.shape[1]), x_t.dtype))
    parts.append(x_t)
    after = total - before - x_t.shape[0]
    if after:
        parts.append(jnp.zeros((after, x_t.shape[1]), x_t.dtype))
    return jnp.concatenate(parts, axis=0)


def set_grads(q_win, do_win, k_pad, v_pad, q_t, k_t, do_t, lse, delta):
    scale = float(HD) ** -0.5
    probs = jnp.exp(dot(q_win, k_pad, 1, 0) * scale - lse)
    d_scores = (probs * (dot(do_win, v_pad, 1, 0) - delta)).astype(BF)
    return (
        dot(k_t, d_scores, 1, 1) * scale,
        dot(q_t, d_scores, 1, 0) * scale,
        dot(do_t, probs.astype(BF), 1, 0),
    )


def local_kernel(q_ref, k_ref, v_ref, do_ref, stat_ref, dq_ref, dk_ref, dv_ref, t_ref):
    q_t, k_t, v_t, do_t = (jnp.transpose(r[...]) for r in (q_ref, k_ref, v_ref, do_ref))
    for h in range(HEADS):
        own = slice(HD * h, HD * (h + 1))
        lo, hi = window(h)
        grads = set_grads(
            q_ref[:, lo:hi],
            do_ref[:, lo:hi],
            padded(k_t[own], HD * h - lo, hi - lo),
            padded(v_t[own], HD * h - lo, hi - lo),
            q_t[own],
            k_t[own],
            do_t[own],
            stat_ref[:, HEADS + h : HEADS + h + 1],
            stat_ref[:, h : h + 1],
        )
        for n, g in enumerate(grads):
            t_ref[n, own, :] = g
    for n, out in enumerate((dq_ref, dk_ref, dv_ref)):
        out[...] = jnp.transpose(t_ref[n])


def packed_grads(lo, hi):
    scale = float(HD) ** -0.5
    one = eye(128)
    x_t = jnp.concatenate([dot(one, lo, 1, 1), dot(one, hi, 1, 1)], axis=0).astype(BF)
    q_t, k_t, v_t, do_t = (x_t[HD * n : HD * (n + 1)] for n in range(4))
    row = iota((64, 256), 0)
    lse = dot(hi, jnp.concatenate([jnp.zeros((64, 256), BF), (row < 3).astype(BF)], axis=0), 1, 0)
    minus = jnp.where((row >= 3) & (row < 6), -1.0, 0.0).astype(BF)
    probs = jnp.exp(dot(lo, padded(k_t, 0, 128), 1, 0) * scale - lse)
    d_probs = dot(hi, jnp.concatenate([jnp.zeros((16, 256), BF), v_t, minus], axis=0), 1, 0)
    d_scores = (probs * d_probs).astype(BF)
    return jnp.concatenate(
        [
            dot(k_t, d_scores, 1, 1) * scale,
            dot(q_t, d_scores, 1, 0) * scale,
            dot(do_t, probs.astype(BF), 1, 0),
        ],
        axis=0,
    )


def sets_kernel(where_ref, in_ref, _, back_ref):
    own = pl.ds(GROUP * where_ref[1], GROUP)
    pairs = in_ref[own, 32:48].astype(F32)
    mine = in_ref[own, 64:80].astype(F32)
    blank = jnp.zeros((GROUP, 16, 56), F32)
    hi = jnp.concatenate(
        [
            jnp.concatenate([pairs[:, :, :64], mine[:, :, 72:80], blank], axis=2),
            jnp.concatenate([pairs[:, :, 64:], mine[:, :, 80:88], blank], axis=2),
        ],
        axis=1,
    )
    group = packed_grads(in_ref[own, :32].reshape(256, 128), hi.reshape(256, 128).astype(BF))
    hi = in_ref[:, 64:80].reshape(256, 128)
    hi = jnp.where(iota((1, 128), 1) < 72, hi, jnp.zeros_like(hi))
    far = packed_grads(in_ref[:, 48:64].reshape(256, 128), hi)
    row = iota((256, 1), 0)
    here = ((row >> 7) == where_ref[1]) & (((row >> 2) & 3) == where_ref[0])
    sel = selector(jnp.where(here, 32 * ((row >> 4) & 7) + (row & 3), -1), 256)
    hi, lo = split(far)
    total = (group + dot(hi, sel, 1, 0) + dot(lo, sel, 1, 0)).astype(BF)
    total = dot(eye(256), total, 1, 1)
    for src in range(GROUP):
        rows = total[32 * src : 32 * (src + 1)]
        back_ref[src, :32] = rows[:, :128].astype(BF)
        tail = [rows[:16, 128:144], rows[16:, 128:144], jnp.zeros((16, 96), F32)]
        back_ref[src, 32:] = jnp.concatenate(tail, axis=1).astype(BF)


def final_kernel(z_ref, dq_ref, dk_ref, dv_ref, oq_ref, ok_ref, ov_ref):
    rows, width = dq_ref.shape
    token = iota((rows, 1), 0)
    perm_t = selector(32 * (token & 7) + 4 * ((token >> 3) & 7) + (token >> 6), rows)
    tail = z_ref[:, 32:].astype(F32)
    tail = jnp.concatenate([tail[:, :, :16], tail[:, :, 16:32]], axis=1).reshape(rows, 16)
    lanes = [z_ref[:, :32].reshape(rows, 128).astype(F32), tail, jnp.zeros((rows, 112), F32)]
    y = dot(perm_t, jnp.concatenate(lanes, axis=1).astype(BF), 1, 0).astype(BF)
    mine = own_head(rows, width)
    for n, (near, out) in enumerate(((dq_ref, oq_ref), (dk_ref, ok_ref), (dv_ref, ov_ref))):
        far = dot(y, (iota((256, 1), 0) - HD * n == lax.rem(iota((1, width), 1), HD)).astype(BF), 1, 0)
        out[...] = (near[...] + jnp.where(mine, far, 0.0)).astype(BF)


def call(kernel, outs, *args, scratch=(), smem=0, hbm=(), flops=0, room=32):
    vmem = pl.BlockSpec(memory_space=pltpu.VMEM)
    far = pl.BlockSpec(memory_space=pltpu.HBM)
    held = far if hbm else vmem
    return pl.pallas_call(
        kernel,
        out_shape=outs,
        in_specs=[pl.BlockSpec(memory_space=pltpu.SMEM)] * smem + [held] * (len(args) - smem),
        out_specs=tuple(far if n in hbm else vmem for n in range(len(outs))) if isinstance(outs, tuple) else vmem,
        scratch_shapes=list(scratch),
        compiler_params=pltpu.CompilerParams(vmem_limit_bytes=room * 1024 * 1024),
        cost_estimate=pl.CostEstimate(flops=flops, bytes_accessed=2_000_000, transcendentals=0),
    )(*args)


def on_device(queries, keys, values, outputs, d_final, stats, w_out):
    q, k, v, o, dy, lse = (x[0] for x in (queries, keys, values, outputs, d_final, stats))
    rows, width = q.shape
    cols = dy.shape[1]
    blocks, ring = lax.axis_size("x"), lax.axis_size(("zh", "zl"))
    shape = jax.ShapeDtypeStruct

    def exchange(x, axes):
        return lax.all_to_all(x, axes, 0, 0, tiled=True)

    ins = (dy, o, w_out, lse.T, q, k, v)
    parts = blocks * CORES
    outs = (
        shape((parts, width * cols // parts // 128 + 8 * HEADS, 128), BF),
        shape((rows, width), BF),
        shape((rows, 256), BF),
        shape((rows, 2 * HEADS), F32),
    )
    out, d_out, pay, stat = call(
        front_kernel,
        outs,
        *ins,
        hbm=(0, 1, 2),
        room=ROOM,
        scratch=[pltpu.VMEM(x.shape, x.dtype) for x in ins + outs[:3]] + [pltpu.SemaphoreType.DMA((11,))],
        flops=1_000_000_000,
    )
    where = jnp.stack([lax.axis_index(a) for a in ("x", "zh", "c")]).astype(jnp.int32)
    over_x = exchange(out, ("x", "c"))
    out = call(mid_kernel, shape((ring, 96, 128), BF), where, over_x, pay, smem=1, flops=100_000_000)
    over_z = exchange(out, ("zh", "zl"))
    near = call(
        local_kernel,
        (shape((rows, width), F32),) * 3,
        q, k, v, d_out, stat,
        scratch=[pltpu.VMEM((3, width, rows), F32)],
        flops=1_000_000_000,
    )
    back = call(sets_kernel, shape((GROUP, 48, 128), BF), where, over_z, near[0], smem=1, flops=200_000_000)
    z = exchange(back, "zl")
    grad = call(weight_kernel, shape((24, 128), F32), over_z, near[0], flops=1_000_000)
    grad = lax.all_gather(grad, ("y", "c"), axis=0)
    grad = call(weight_end_kernel, shape((width // (blocks * ring), cols), F32), grad, flops=1_000_000)
    d_q, d_k, d_v = call(final_kernel, (shape((rows, width), BF),) * 3, z, *near, flops=300_000_000)
    return d_q[None], d_k[None], d_v[None], grad


def solution(mesh):
    dp, seq = mesh.devices.shape
    fine = jax.sharding.Mesh(
        mesh.devices.reshape(dp // CORES, CORES, seq // 16, 16 // GROUP, GROUP), ("y", "c", "x", "zh", "zl")
    )
    dp_axes, seq_axes = ("y", "c"), ("x", "zh", "zl")
    placed = P(dp_axes, seq_axes, None)
    return jax.shard_map(
        on_device,
        mesh=fine,
        in_specs=(placed,) * 6 + (P(),),
        out_specs=(placed,) * 3 + (P(seq_axes, None),),
        check_vma=False,
    )
```

```python
import functools

import jax
import jax.numpy as jnp
from jax import lax
from jax.experimental import pallas as pl
from jax.experimental.pallas import tpu as pltpu
from jax.sharding import PartitionSpec as P

HEADS = 8
HD = 48
GROUP = 8
CORES = 2
ROOM = 60
BF = jnp.bfloat16
F32 = jnp.float32


def iota(shape, dim):
    return lax.broadcasted_iota(jnp.int32, shape, dim)


def dot(a, b, ca, cb):
    return lax.dot_general(a, b, (((ca,), (cb,)), ((), ())), preferred_element_type=F32)


def split(x):
    hi = x.astype(BF)
    return hi, (x - hi.astype(F32)).astype(BF)


def eye(n):
    return (iota((n, n), 0) == iota((n, n), 1)).astype(BF)


def packed_token(p):
    return 64 * (p & 3) + 8 * ((p >> 2) & 7) + (p >> 5)


def spread(part, lanes, width):
    return (iota((1, lanes), 1) - HD * part == lax.rem(iota((width, 1), 0), HD)).astype(BF)


def own_head(rows, width):
    return lax.div(iota((1, width), 1), HD) == (iota((rows, 1), 0) & (GROUP - 1))


def selector(source, count):
    return (iota((source.shape[0], count), 1) == source).astype(BF)


def front_kernel(*refs):
    hbm, (out_ref, do_ref, pay_ref, stat_ref), vmem, sems = refs[:7], refs[7:11], refs[11:18], refs[18]
    copies = [pltpu.make_async_copy(a, b, sems.at[n]) for n, (a, b) in enumerate(zip(hbm, vmem))]
    for copy in copies:
        copy.start()
    dy_ref, o_ref, w_ref, lse_ref, q_ref, k_ref, v_ref = vmem
    rows, width = o_ref.shape
    cols = dy_ref.shape[1]
    parts = out_ref.shape[0]
    count = width * cols // parts // 128
    for copy in copies:
        copy.wait()
    out, dy = o_ref[...], dy_ref[...]
    d_out = dot(dy, w_ref[...], 1, 1).astype(BF)
    do_ref[...] = d_out
    hi, lo = split(d_out.astype(F32) * out.astype(F32))
    heads = (lax.div(iota((width, 1), 0), HD) == iota((width, 128), 1)).astype(BF)
    delta = (dot(hi, heads, 1, 0) + dot(lo, heads, 1, 0))[:, :HEADS]
    lse = jnp.transpose(lse_ref[...])
    stat_ref[...] = jnp.concatenate([delta, lse], axis=1)
    mine = own_head(rows, width)
    pay = jnp.zeros((rows, 256), F32)
    for part, x in enumerate((q_ref[...], k_ref[...], v_ref[...], d_out)):
        pay += dot(jnp.where(mine, x, jnp.zeros_like(x)), spread(part, 256, width), 1, 0)
    pick = iota((1, HEADS), 1) == (iota((rows, 1), 0) & (GROUP - 1))
    lane = iota((rows, 128), 1)
    tail = pay[:, 128:]
    for base, x in ((64, lse), (67, delta)):
        own = jnp.sum(jnp.where(pick, x, 0.0), axis=1, keepdims=True)
        for n in range(3):
            piece = own.astype(BF).astype(F32)
            tail += jnp.where(lane == base + n, piece, 0.0)
            own = own - piece
    pay = jnp.concatenate([pay[:, :128], tail], axis=1).astype(BF)
    pay_ref[...] = dot(selector(packed_token(iota((rows, 1), 0)), rows), pay, 1, 0).astype(BF)
    at = iota((8 * HEADS, 1), 0)
    token = 64 * (at & 3) + ((at >> 2) & 7)
    first = selector(jnp.where(at < 4 * HEADS, token, -1), rows)
    second = selector(jnp.where(at < 4 * HEADS, -1, token), rows)
    top = (dot(first, pay[:, :128], 1, 0) + dot(second, pay[:, 128:], 1, 0)).astype(BF)
    for n in range(parts):
        out_ref[n, count:] = top
    each, half = width * CORES // parts, cols // CORES
    grad = dot(out, dy, 0, 0)
    for n in range(parts):
        x, c = divmod(n, CORES)
        for t in range(half // 128):
            tile = grad[each * x : each * (x + 1), half * c + 128 * t : half * c + 128 * (t + 1)]
            out_ref[n, each * t : each * (t + 1)] = tile.astype(BF)


def mid_kernel(where_ref, in_ref, pay_ref, _, out_ref):
    ring = out_ref.shape[0]
    count = in_ref.shape[1] - 8 * HEADS
    sums = jnp.sum(in_ref[:, :count].astype(F32), axis=0).astype(BF)
    each = count // 3
    few = each // ring
    to = iota((16 * ring, 1), 0)
    z, q = to >> 4, to & 15
    t = (q * 43) >> 8
    main = dot(selector(each * t + few * z + q - few * t, count), sums, 1, 0).astype(BF)
    last = selector(jnp.where(q < 8, 2 * each + few * z + 4 + (q & 1), -1), count)
    last = dot(last, sums, 1, 0)
    lane = iota((1, 128), 1)
    last = jnp.where((lane >> 5) == (q >> 1), last, 0.0).astype(BF)
    last = dot(last, selector(96 + (iota((128, 1), 0) & 31), 128), 1, 0)
    top = jnp.concatenate([in_ref[CORES * x + where_ref[2], count:] for x in range(4)], axis=0)
    to = iota((top.shape[0], 1), 0)
    source = 64 * ((to >> 2) & 3) + 32 * ((to >> 4) & 1) + 4 * (to >> 5) + (to & 3)
    top = dot(selector(source, top.shape[0]), top, 1, 0)
    for r in range(GROUP):
        low = pay_ref[32 * r : 32 * (r + 1), :128]
        rest = pay_ref[32 * r : 32 * (r + 1), 128:].astype(F32)
        pairs = jnp.concatenate([rest[:16, :64], rest[16:, :64]], axis=1).astype(BF)
        near = top[32 * r : 32 * r + 16].astype(BF)
        mixed = [top[32 * r + 16 : 32 * (r + 1), :72], rest[:16, 64:72], rest[16:, 64:72], jnp.zeros((16, 40), F32)]
        mixed = jnp.concatenate(mixed, axis=1)
        for z in range(r, ring, GROUP):
            out_ref[z, :32] = low
            out_ref[z, 32:48] = pairs
            out_ref[z, 48:64] = near
            out_ref[z, 64:80] = (mixed + last[16 * z : 16 * (z + 1)]).astype(BF)
            out_ref[z, 80:] = main[16 * z : 16 * (z + 1)]


def weight_kernel(in_ref, out_ref):
    out_ref[:16] = jnp.sum(in_ref[:, 80:].astype(F32), axis=0)
    out_ref[16:] = jnp.sum(in_ref[:, 64:80].astype(F32), axis=0)[:8]


def weight_end_kernel(in_ref, out_ref):
    each = out_ref.shape[0]
    parts = []
    for c in range(CORES):
        total = in_ref[c]
        for y in range(1, in_ref.shape[0] // CORES):
            total = total + in_ref[CORES * y + c]
        last = jnp.concatenate([total[16 + 2 * k : 18 + 2 * k, 96:] for k in range(4)], axis=1)
        total = jnp.concatenate([total[:16], last], axis=0)
        parts += [total[each * t : each * (t + 1)] for t in range(3)]
    out_ref[...] = jnp.concatenate(parts, axis=1)


def window(h):
    lo = HD * h // 128 * 128
    hi = -(-HD * (h + 1) // 128) * 128
    return lo, hi


def padded(x_t, before, total):
    parts = []
    if before:
        parts.append(jnp.zeros((before, x_t.shape[1]), x_t.dtype))
    parts.append(x_t)
    after = total - before - x_t.shape[0]
    if after:
        parts.append(jnp.zeros((after, x_t.shape[1]), x_t.dtype))
    return jnp.concatenate(parts, axis=0)


def set_grads(q_win, do_win, k_pad, v_pad, q_t, k_t, do_t, lse, delta):
    scale = float(HD) ** -0.5
    probs = jnp.exp(dot(q_win, k_pad, 1, 0) * scale - lse)
    d_scores = (probs * (dot(do_win, v_pad, 1, 0) - delta)).astype(BF)
    return (
        dot(k_t, d_scores, 1, 1) * scale,
        dot(q_t, d_scores, 1, 0) * scale,
        dot(do_t, probs.astype(BF), 1, 0),
    )


def local_kernel(q_ref, k_ref, v_ref, do_ref, stat_ref, dq_ref, dk_ref, dv_ref, t_ref):
    q_t, k_t, v_t, do_t = (jnp.transpose(r[...]) for r in (q_ref, k_ref, v_ref, do_ref))
    for h in range(HEADS):
        own = slice(HD * h, HD * (h + 1))
        lo, hi = window(h)
        grads = set_grads(
            q_ref[:, lo:hi],
            do_ref[:, lo:hi],
            padded(k_t[own], HD * h - lo, hi - lo),
            padded(v_t[own], HD * h - lo, hi - lo),
            q_t[own],
            k_t[own],
            do_t[own],
            stat_ref[:, HEADS + h : HEADS + h + 1],
            stat_ref[:, h : h + 1],
        )
        for n, g in enumerate(grads):
            t_ref[n, own, :] = g
    for n, out in enumerate((dq_ref, dk_ref, dv_ref)):
        out[...] = jnp.transpose(t_ref[n])


def packed_grads(lo, hi):
    scale = float(HD) ** -0.5
    one = eye(128)
    x_t = jnp.concatenate([dot(one, lo, 1, 1), dot(one, hi, 1, 1)], axis=0).astype(BF)
    q_t, k_t, v_t, do_t = (x_t[HD * n : HD * (n + 1)] for n in range(4))
    row = iota((64, 256), 0)
    lse = dot(hi, jnp.concatenate([jnp.zeros((64, 256), BF), (row < 3).astype(BF)], axis=0), 1, 0)
    minus = jnp.where((row >= 3) & (row < 6), -1.0, 0.0).astype(BF)
    probs = jnp.exp(dot(lo, padded(k_t, 0, 128), 1, 0) * scale - lse)
    d_probs = dot(hi, jnp.concatenate([jnp.zeros((16, 256), BF), v_t, minus], axis=0), 1, 0)
    d_scores = (probs * d_probs).astype(BF)
    return jnp.concatenate(
        [
            dot(k_t, d_scores, 1, 1) * scale,
            dot(q_t, d_scores, 1, 0) * scale,
            dot(do_t, probs.astype(BF), 1, 0),
        ],
        axis=0,
    )


def sets_kernel(where_ref, in_ref, back_ref):
    own = pl.ds(GROUP * where_ref[1], GROUP)
    pairs = in_ref[own, 32:48].astype(F32)
    mine = in_ref[own, 64:80].astype(F32)
    blank = jnp.zeros((GROUP, 16, 56), F32)
    hi = jnp.concatenate(
        [
            jnp.concatenate([pairs[:, :, :64], mine[:, :, 72:80], blank], axis=2),
            jnp.concatenate([pairs[:, :, 64:], mine[:, :, 80:88], blank], axis=2),
        ],
        axis=1,
    )
    group = packed_grads(in_ref[own, :32].reshape(256, 128), hi.reshape(256, 128).astype(BF))
    hi = in_ref[:, 64:80].reshape(256, 128)
    hi = jnp.where(iota((1, 128), 1) < 72, hi, jnp.zeros_like(hi))
    far = packed_grads(in_ref[:, 48:64].reshape(256, 128), hi)
    row = iota((256, 1), 0)
    here = ((row >> 7) == where_ref[1]) & (((row >> 2) & 3) == where_ref[0])
    sel = selector(jnp.where(here, 32 * ((row >> 4) & 7) + (row & 3), -1), 256)
    hi, lo = split(far)
    total = (group + dot(hi, sel, 1, 0) + dot(lo, sel, 1, 0)).astype(BF)
    total = dot(eye(256), total, 1, 1)
    for src in range(GROUP):
        rows = total[32 * src : 32 * (src + 1)]
        back_ref[src, :32] = rows[:, :128].astype(BF)
        tail = [rows[:16, 128:144], rows[16:, 128:144], jnp.zeros((16, 96), F32)]
        back_ref[src, 32:] = jnp.concatenate(tail, axis=1).astype(BF)


def final_kernel(z_ref, dq_ref, dk_ref, dv_ref, oq_ref, ok_ref, ov_ref):
    rows, width = dq_ref.shape
    token = iota((rows, 1), 0)
    perm_t = selector(32 * (token & 7) + 4 * ((token >> 3) & 7) + (token >> 6), rows)
    tail = z_ref[:, 32:].astype(F32)
    tail = jnp.concatenate([tail[:, :, :16], tail[:, :, 16:32]], axis=1).reshape(rows, 16)
    lanes = [z_ref[:, :32].reshape(rows, 128).astype(F32), tail, jnp.zeros((rows, 112), F32)]
    y = dot(perm_t, jnp.concatenate(lanes, axis=1).astype(BF), 1, 0).astype(BF)
    mine = own_head(rows, width)
    for n, (near, out) in enumerate(((dq_ref, oq_ref), (dk_ref, ok_ref), (dv_ref, ov_ref))):
        far = dot(y, (iota((256, 1), 0) - HD * n == lax.rem(iota((1, width), 1), HD)).astype(BF), 1, 0)
        out[...] = (near[...] + jnp.where(mine, far, 0.0)).astype(BF)


def call(kernel, outs, *args, scratch=(), smem=0, hbm=False, flops=0, room=32):
    vmem = pl.BlockSpec(memory_space=pltpu.VMEM)
    held = pl.BlockSpec(memory_space=pltpu.HBM) if hbm else vmem
    return pl.pallas_call(
        kernel,
        out_shape=outs,
        in_specs=[pl.BlockSpec(memory_space=pltpu.SMEM)] * smem + [held] * (len(args) - smem),
        out_specs=jax.tree.map(lambda _: vmem, outs),
        scratch_shapes=list(scratch),
        compiler_params=pltpu.CompilerParams(vmem_limit_bytes=room * 1024 * 1024),
        cost_estimate=pl.CostEstimate(flops=flops, bytes_accessed=2_000_000, transcendentals=0),
    )(*args)


def on_device(queries, keys, values, outputs, d_final, stats, w_out):
    q, k, v, o, dy, lse = (x[0] for x in (queries, keys, values, outputs, d_final, stats))
    rows, width = q.shape
    cols = dy.shape[1]
    blocks, ring = lax.axis_size("x"), lax.axis_size(("zh", "zl"))
    shape = jax.ShapeDtypeStruct

    def exchange(x, axes):
        return lax.all_to_all(x, axes, 0, 0, tiled=True)

    ins = (dy, o, w_out, lse.T, q, k, v)
    parts = blocks * CORES
    outs = (
        shape((parts, width * cols // parts // 128 + 8 * HEADS, 128), BF),
        shape((rows, width), BF),
        shape((rows, 256), BF),
        shape((rows, 2 * HEADS), F32),
    )
    out, d_out, pay, stat = call(
        front_kernel,
        outs,
        *ins,
        hbm=True,
        room=ROOM,
        scratch=[pltpu.VMEM(x.shape, x.dtype) for x in ins] + [pltpu.SemaphoreType.DMA((len(ins),))],
        flops=1_000_000_000,
    )
    where = jnp.stack([lax.axis_index(a) for a in ("x", "zh", "c")]).astype(jnp.int32)
    over_x = exchange(out, ("x", "c"))
    near = call(
        local_kernel,
        (shape((rows, width), F32),) * 3,
        q, k, v, d_out, stat,
        scratch=[pltpu.VMEM((3, width, rows), F32)],
        flops=1_000_000_000,
    )
    out = call(mid_kernel, shape((ring, 96, 128), BF), where, over_x, pay, near[0], smem=1, flops=100_000_000)
    over_z = exchange(out, ("zh", "zl"))
    back = call(sets_kernel, shape((GROUP, 48, 128), BF), where, over_z, smem=1, flops=200_000_000)
    z = exchange(back, "zl")
    grad = call(weight_kernel, shape((24, 128), F32), over_z, flops=1_000_000)
    grad = lax.all_gather(grad, ("y", "c"), axis=0)
    grad = call(weight_end_kernel, shape((width // (blocks * ring), cols), F32), grad, flops=1_000_000)
    d_q, d_k, d_v = call(final_kernel, (shape((rows, width), BF),) * 3, z, *near, flops=300_000_000)
    return d_q[None], d_k[None], d_v[None], grad


def solution(mesh):
    dp, seq = mesh.devices.shape
    fine = jax.sharding.Mesh(
        mesh.devices.reshape(dp // CORES, CORES, seq // 16, 16 // GROUP, GROUP), ("y", "c", "x", "zh", "zl")
    )
    dp_axes, seq_axes = ("y", "c"), ("x", "zh", "zl")
    placed = P(dp_axes, seq_axes, None)
    return jax.shard_map(
        on_device,
        mesh=fine,
        in_specs=(placed,) * 6 + (P(),),
        out_specs=(placed,) * 3 + (P(seq_axes, None),),
        check_vma=False,
    )
```

```python
import functools

import jax
import jax.numpy as jnp
from jax import lax
from jax.experimental import pallas as pl
from jax.experimental.pallas import tpu as pltpu
from jax.sharding import PartitionSpec as P

HEADS = 8
HD = 48
GROUP = 8
CORES = 2
ROOM = 60
BF = jnp.bfloat16
F32 = jnp.float32


def iota(shape, dim):
    return lax.broadcasted_iota(jnp.int32, shape, dim)


def dot(a, b, ca, cb):
    return lax.dot_general(a, b, (((ca,), (cb,)), ((), ())), preferred_element_type=F32)


def split(x):
    hi = x.astype(BF)
    return hi, (x - hi.astype(F32)).astype(BF)


def eye(n):
    return (iota((n, n), 0) == iota((n, n), 1)).astype(BF)


def packed_token(p):
    return 64 * (p & 3) + 8 * ((p >> 2) & 7) + (p >> 5)


def spread(part, lanes, width):
    return (iota((1, lanes), 1) - HD * part == lax.rem(iota((width, 1), 0), HD)).astype(BF)


def own_head(rows, width):
    return lax.div(iota((1, width), 1), HD) == (iota((rows, 1), 0) & (GROUP - 1))


def selector(source, count):
    return (iota((source.shape[0], count), 1) == source).astype(BF)


def front_kernel(*refs):
    hbm, (out_ref, do_ref, pay_ref, stat_ref), vmem, sems = refs[:7], refs[7:11], refs[11:18], refs[18]
    copies = [pltpu.make_async_copy(a, b, sems.at[n]) for n, (a, b) in enumerate(zip(hbm, vmem))]
    for copy in copies:
        copy.start()
    dy_ref, o_ref, w_ref, lse_ref, q_ref, k_ref, v_ref = vmem
    rows, width = o_ref.shape
    cols = dy_ref.shape[1]
    parts = out_ref.shape[0]
    count = width * cols // parts // 128
    for copy in copies:
        copy.wait()
    out, dy = o_ref[...], dy_ref[...]
    d_out = dot(dy, w_ref[...], 1, 1).astype(BF)
    do_ref[...] = d_out
    hi, lo = split(d_out.astype(F32) * out.astype(F32))
    heads = (lax.div(iota((width, 1), 0), HD) == iota((width, 128), 1)).astype(BF)
    delta = (dot(hi, heads, 1, 0) + dot(lo, heads, 1, 0))[:, :HEADS]
    lse = jnp.transpose(lse_ref[...])
    stat_ref[...] = jnp.concatenate([delta, lse], axis=1)
    mine = own_head(rows, width)
    pay = jnp.zeros((rows, 256), F32)
    for part, x in enumerate((q_ref[...], k_ref[...], v_ref[...], d_out)):
        pay += dot(jnp.where(mine, x, jnp.zeros_like(x)), spread(part, 256, width), 1, 0)
    pick = iota((1, HEADS), 1) == (iota((rows, 1), 0) & (GROUP - 1))
    lane = iota((rows, 128), 1)
    tail = pay[:, 128:]
    for base, x in ((64, lse), (67, delta)):
        own = jnp.sum(jnp.where(pick, x, 0.0), axis=1, keepdims=True)
        for n in range(3):
            piece = own.astype(BF).astype(F32)
            tail += jnp.where(lane == base + n, piece, 0.0)
            own = own - piece
    pay = jnp.concatenate([pay[:, :128], tail], axis=1).astype(BF)
    pay_ref[...] = pay
    at = iota((8 * HEADS, 1), 0)
    token = 64 * (at & 3) + ((at >> 2) & 7)
    first = selector(jnp.where(at < 4 * HEADS, token, -1), rows)
    second = selector(jnp.where(at < 4 * HEADS, -1, token), rows)
    top = (dot(first, pay[:, :128], 1, 0) + dot(second, pay[:, 128:], 1, 0)).astype(BF)
    for n in range(parts):
        out_ref[n, count:] = top
    each, half = width * CORES // parts, cols // CORES
    grad = dot(out, dy, 0, 0)
    for n in range(parts):
        x, c = divmod(n, CORES)
        for t in range(half // 128):
            tile = grad[each * x : each * (x + 1), half * c + 128 * t : half * c + 128 * (t + 1)]
            out_ref[n, each * t : each * (t + 1)] = tile.astype(BF)


def pack_kernel(pay_ref, out_ref):
    rows = pay_ref.shape[0]
    pay = dot(selector(packed_token(iota((rows, 1), 0)), rows), pay_ref[...], 1, 0)
    for r in range(GROUP):
        low = pay[32 * r : 32 * (r + 1), :128]
        rest = pay[32 * r : 32 * (r + 1), 128:]
        out_ref[r, :32] = low.astype(BF)
        out_ref[r, 32:48] = jnp.concatenate([rest[:16, :64], rest[16:, :64]], axis=1).astype(BF)
        stats = [jnp.zeros((16, 72), F32), rest[:16, 64:72], rest[16:, 64:72], jnp.zeros((16, 40), F32)]
        out_ref[r, 48:] = jnp.concatenate(stats, axis=1).astype(BF)


def mid_kernel(where_ref, in_ref, pay_ref, _, out_ref):
    ring = out_ref.shape[0]
    count = in_ref.shape[1] - 8 * HEADS
    sums = jnp.sum(in_ref[:, :count].astype(F32), axis=0).astype(BF)
    each = count // 3
    few = each // ring
    to = iota((16 * ring, 1), 0)
    z, q = to >> 4, to & 15
    t = (q * 43) >> 8
    main = dot(selector(each * t + few * z + q - few * t, count), sums, 1, 0).astype(BF)
    last = selector(jnp.where(q < 8, 2 * each + few * z + 4 + (q & 1), -1), count)
    last = dot(last, sums, 1, 0)
    lane = iota((1, 128), 1)
    last = jnp.where((lane >> 5) == (q >> 1), last, 0.0).astype(BF)
    last = dot(last, selector(96 + (iota((128, 1), 0) & 31), 128), 1, 0)
    top = jnp.concatenate([in_ref[CORES * x + where_ref[2], count:] for x in range(4)], axis=0)
    to = iota((top.shape[0], 1), 0)
    source = 64 * ((to >> 2) & 3) + 32 * ((to >> 4) & 1) + 4 * (to >> 5) + (to & 3)
    top = dot(selector(source, top.shape[0]), top, 1, 0)
    lane = iota((1, 128), 1)
    for r in range(GROUP):
        near = top[32 * r : 32 * r + 16].astype(BF)
        mixed = jnp.where(lane < 72, top[32 * r + 16 : 32 * (r + 1)], 0.0) + pay_ref[r, 48:].astype(F32)
        for z in range(r, ring, GROUP):
            out_ref[z, :48] = pay_ref[r, :48]
            out_ref[z, 48:64] = near
            out_ref[z, 64:80] = (mixed + last[16 * z : 16 * (z + 1)]).astype(BF)
            out_ref[z, 80:] = main[16 * z : 16 * (z + 1)]


def weight_end(in_ref, out_ref):
    each = out_ref.shape[0]
    parts = []
    for c in range(CORES):
        total = in_ref[c]
        for y in range(1, in_ref.shape[0] // CORES):
            total = total + in_ref[CORES * y + c]
        last = jnp.concatenate([total[16 + 2 * k : 18 + 2 * k, 96:] for k in range(4)], axis=1)
        total = jnp.concatenate([total[:16], last], axis=0)
        parts += [total[each * t : each * (t + 1)] for t in range(3)]
    out_ref[...] = jnp.concatenate(parts, axis=1)


def window(h):
    lo = HD * h // 128 * 128
    hi = -(-HD * (h + 1) // 128) * 128
    return lo, hi


def padded(x_t, before, total):
    parts = []
    if before:
        parts.append(jnp.zeros((before, x_t.shape[1]), x_t.dtype))
    parts.append(x_t)
    after = total - before - x_t.shape[0]
    if after:
        parts.append(jnp.zeros((after, x_t.shape[1]), x_t.dtype))
    return jnp.concatenate(parts, axis=0)


def set_grads(q_win, do_win, k_pad, v_pad, q_t, k_t, do_t, lse, delta):
    scale = float(HD) ** -0.5
    probs = jnp.exp(dot(q_win, k_pad, 1, 0) * scale - lse)
    d_scores = (probs * (dot(do_win, v_pad, 1, 0) - delta)).astype(BF)
    return (
        dot(k_t, d_scores, 1, 1) * scale,
        dot(q_t, d_scores, 1, 0) * scale,
        dot(do_t, probs.astype(BF), 1, 0),
    )


def local_kernel(q_ref, k_ref, v_ref, do_ref, stat_ref, dq_ref, dk_ref, dv_ref, t_ref):
    q_t, k_t, v_t, do_t = (jnp.transpose(r[...]) for r in (q_ref, k_ref, v_ref, do_ref))
    for h in range(HEADS):
        own = slice(HD * h, HD * (h + 1))
        lo, hi = window(h)
        grads = set_grads(
            q_ref[:, lo:hi],
            do_ref[:, lo:hi],
            padded(k_t[own], HD * h - lo, hi - lo),
            padded(v_t[own], HD * h - lo, hi - lo),
            q_t[own],
            k_t[own],
            do_t[own],
            stat_ref[:, HEADS + h : HEADS + h + 1],
            stat_ref[:, h : h + 1],
        )
        for n, g in enumerate(grads):
            t_ref[n, own, :] = g
    for n, out in enumerate((dq_ref, dk_ref, dv_ref)):
        out[...] = jnp.transpose(t_ref[n])


def packed_grads(lo, hi):
    scale = float(HD) ** -0.5
    one = eye(128)
    x_t = jnp.concatenate([dot(one, lo, 1, 1), dot(one, hi, 1, 1)], axis=0).astype(BF)
    q_t, k_t, v_t, do_t = (x_t[HD * n : HD * (n + 1)] for n in range(4))
    row = iota((64, 256), 0)
    lse = dot(hi, jnp.concatenate([jnp.zeros((64, 256), BF), (row < 3).astype(BF)], axis=0), 1, 0)
    minus = jnp.where((row >= 3) & (row < 6), -1.0, 0.0).astype(BF)
    probs = jnp.exp(dot(lo, padded(k_t, 0, 128), 1, 0) * scale - lse)
    d_probs = dot(hi, jnp.concatenate([jnp.zeros((16, 256), BF), v_t, minus], axis=0), 1, 0)
    d_scores = (probs * d_probs).astype(BF)
    return jnp.concatenate(
        [
            dot(k_t, d_scores, 1, 1) * scale,
            dot(q_t, d_scores, 1, 0) * scale,
            dot(do_t, probs.astype(BF), 1, 0),
        ],
        axis=0,
    )


def sets_kernel(where_ref, in_ref, back_ref, grad_ref):
    grad_ref[:16] = jnp.sum(in_ref[:, 80:].astype(F32), axis=0)
    grad_ref[16:] = jnp.sum(in_ref[:, 64:80].astype(F32), axis=0)[:8]
    own = pl.ds(GROUP * where_ref[1], GROUP)
    pairs = in_ref[own, 32:48].astype(F32)
    mine = in_ref[own, 64:80].astype(F32)
    blank = jnp.zeros((GROUP, 16, 56), F32)
    hi = jnp.concatenate(
        [
            jnp.concatenate([pairs[:, :, :64], mine[:, :, 72:80], blank], axis=2),
            jnp.concatenate([pairs[:, :, 64:], mine[:, :, 80:88], blank], axis=2),
        ],
        axis=1,
    )
    group = packed_grads(in_ref[own, :32].reshape(256, 128), hi.reshape(256, 128).astype(BF))
    hi = in_ref[:, 64:80].reshape(256, 128)
    hi = jnp.where(iota((1, 128), 1) < 72, hi, jnp.zeros_like(hi))
    far = packed_grads(in_ref[:, 48:64].reshape(256, 128), hi)
    token, far_token = iota((256, 1), 0), iota((1, 256), 1)
    match = 128 * where_ref[1] + 16 * (token >> 5) + 4 * where_ref[0] + (token & 3)
    sel = ((far_token == match) & ((token & 31) < 4)).astype(BF)
    turn = jnp.concatenate([eye(256), sel], axis=1)
    hi, lo = split(jnp.concatenate([group, far], axis=1))
    total = dot(turn, hi, 1, 1) + dot(turn, lo, 1, 1)
    for src in range(GROUP):
        rows = total[32 * src : 32 * (src + 1)]
        back_ref[src, :32] = rows[:, :128].astype(BF)
        tail = [rows[:16, 128:144], rows[16:, 128:144], jnp.zeros((16, 96), F32)]
        back_ref[src, 32:] = jnp.concatenate(tail, axis=1).astype(BF)


def final_kernel(z_ref, dq_ref, dk_ref, dv_ref, grad_ref, oq_ref, ok_ref, ov_ref, ow_ref):
    weight_end(grad_ref, ow_ref)
    rows, width = dq_ref.shape
    token = iota((rows, 1), 0)
    perm_t = selector(32 * (token & 7) + 4 * ((token >> 3) & 7) + (token >> 6), rows)
    tail = z_ref[:, 32:].astype(F32)
    tail = jnp.concatenate([tail[:, :, :16], tail[:, :, 16:32]], axis=1).reshape(rows, 16)
    lanes = [z_ref[:, :32].reshape(rows, 128).astype(F32), tail, jnp.zeros((rows, 112), F32)]
    y = dot(perm_t, jnp.concatenate(lanes, axis=1).astype(BF), 1, 0).astype(BF)
    mine = own_head(rows, width)
    for n, (near, out) in enumerate(((dq_ref, oq_ref), (dk_ref, ok_ref), (dv_ref, ov_ref))):
        far = dot(y, (iota((256, 1), 0) - HD * n == lax.rem(iota((1, width), 1), HD)).astype(BF), 1, 0)
        out[...] = (near[...] + jnp.where(mine, far, 0.0)).astype(BF)


def call(kernel, outs, *args, scratch=(), smem=0, hbm=False, flops=0, room=32):
    vmem = pl.BlockSpec(memory_space=pltpu.VMEM)
    held = pl.BlockSpec(memory_space=pltpu.HBM) if hbm else vmem
    return pl.pallas_call(
        kernel,
        out_shape=outs,
        in_specs=[pl.BlockSpec(memory_space=pltpu.SMEM)] * smem + [held] * (len(args) - smem),
        out_specs=jax.tree.map(lambda _: vmem, outs),
        scratch_shapes=list(scratch),
        compiler_params=pltpu.CompilerParams(vmem_limit_bytes=room * 1024 * 1024),
        cost_estimate=pl.CostEstimate(flops=flops, bytes_accessed=2_000_000, transcendentals=0),
    )(*args)


def on_device(queries, keys, values, outputs, d_final, stats, w_out):
    q, k, v, o, dy, lse = (x[0] for x in (queries, keys, values, outputs, d_final, stats))
    rows, width = q.shape
    cols = dy.shape[1]
    blocks, ring = lax.axis_size("x"), lax.axis_size(("zh", "zl"))
    shape = jax.ShapeDtypeStruct

    def exchange(x, axes):
        return lax.all_to_all(x, axes, 0, 0, tiled=True)

    ins = (dy, o, w_out, lse.T, q, k, v)
    parts = blocks * CORES
    outs = (
        shape((parts, width * cols // parts // 128 + 8 * HEADS, 128), BF),
        shape((rows, width), BF),
        shape((rows, 256), BF),
        shape((rows, 2 * HEADS), F32),
    )
    out, d_out, pay, stat = call(
        front_kernel,
        outs,
        *ins,
        hbm=True,
        room=ROOM,
        scratch=[pltpu.VMEM(x.shape, x.dtype) for x in ins] + [pltpu.SemaphoreType.DMA((len(ins),))],
        flops=1_000_000_000,
    )
    where = jnp.stack([lax.axis_index(a) for a in ("x", "zh", "c")]).astype(jnp.int32)
    over_x = exchange(out, ("x", "c"))
    pay = call(pack_kernel, shape((GROUP, 64, 128), BF), pay, flops=100_000_000)
    near = call(
        local_kernel,
        (shape((rows, width), F32),) * 3,
        q, k, v, d_out, stat,
        scratch=[pltpu.VMEM((3, width, rows), F32)],
        flops=1_000_000_000,
    )
    out = call(mid_kernel, shape((ring, 96, 128), BF), where, over_x, pay, near[0], smem=1, flops=100_000_000)
    over_z = exchange(out, ("zh", "zl"))
    back, grad = call(
        sets_kernel, (shape((GROUP, 48, 128), BF), shape((24, 128), F32)), where, over_z, smem=1, flops=200_000_000
    )
    z = exchange(back, "zl")
    grad = lax.all_gather(grad, ("y", "c"), axis=0)
    d_q, d_k, d_v, grad = call(
        final_kernel,
        (shape((rows, width), BF),) * 3 + (shape((width // (blocks * ring), cols), F32),),
        z, *near, grad,
        flops=300_000_000,
    )
    return d_q[None], d_k[None], d_v[None], grad


def solution(mesh):
    dp, seq = mesh.devices.shape
    fine = jax.sharding.Mesh(
        mesh.devices.reshape(dp // CORES, CORES, seq // 16, 16 // GROUP, GROUP), ("y", "c", "x", "zh", "zl")
    )
    dp_axes, seq_axes = ("y", "c"), ("x", "zh", "zl")
    placed = P(dp_axes, seq_axes, None)
    return jax.shard_map(
        on_device,
        mesh=fine,
        in_specs=(placed,) * 6 + (P(),),
        out_specs=(placed,) * 3 + (P(seq_axes, None),),
        check_vma=False,
    )
```

```python
import functools

import jax
import jax.numpy as jnp
from jax import lax
from jax.experimental import pallas as pl
from jax.experimental.pallas import tpu as pltpu
from jax.sharding import PartitionSpec as P

HEADS = 8
HD = 48
GROUP = 8
CORES = 2
ROOM = 60
BF = jnp.bfloat16
F32 = jnp.float32


def iota(shape, dim):
    return lax.broadcasted_iota(jnp.int32, shape, dim)


def dot(a, b, ca, cb):
    return lax.dot_general(a, b, (((ca,), (cb,)), ((), ())), preferred_element_type=F32)


def split(x):
    hi = x.astype(BF)
    return hi, (x - hi.astype(F32)).astype(BF)


def eye(n):
    return (iota((n, n), 0) == iota((n, n), 1)).astype(BF)


def packed_token(p):
    return 64 * (p & 3) + 8 * ((p >> 2) & 7) + (p >> 5)


def spread(part, lanes, width):
    return (iota((1, lanes), 1) - HD * part == lax.rem(iota((width, 1), 0), HD)).astype(BF)


def own_head(rows, width):
    return lax.div(iota((1, width), 1), HD) == (iota((rows, 1), 0) & (GROUP - 1))


def selector(source, count):
    return (iota((source.shape[0], count), 1) == source).astype(BF)


def stat_lanes(x):
    row, lane = iota((128, 1), 0), iota((1, 128), 1)
    return dot(x, ((row >= 64) & (row < 72) & ((row & 7) == (lane & 7))).astype(BF), 1, 0)


def stat_rows(rows_of, source, group):
    x = dot(selector(source, rows_of.shape[0]), rows_of, 1, 0)
    return jnp.where((iota((1, 128), 1) >> 3) == group, x, 0.0).astype(BF)


def front_kernel(*refs):
    hbm, (out_ref, do_ref, pay_ref, stat_ref), vmem, sems = refs[:7], refs[7:11], refs[11:18], refs[18]
    copies = [pltpu.make_async_copy(a, b, sems.at[n]) for n, (a, b) in enumerate(zip(hbm, vmem))]
    for copy in copies:
        copy.start()
    dy_ref, o_ref, w_ref, lse_ref, q_ref, k_ref, v_ref = vmem
    rows, width = o_ref.shape
    cols = dy_ref.shape[1]
    parts = out_ref.shape[0]
    count = width * cols // parts // 128
    for copy in copies:
        copy.wait()
    out, dy = o_ref[...], dy_ref[...]
    d_out = dot(dy, w_ref[...], 1, 1).astype(BF)
    do_ref[...] = d_out
    hi, lo = split(d_out.astype(F32) * out.astype(F32))
    heads = (lax.div(iota((width, 1), 0), HD) == iota((width, 128), 1)).astype(BF)
    delta = (dot(hi, heads, 1, 0) + dot(lo, heads, 1, 0))[:, :HEADS]
    lse = jnp.transpose(lse_ref[...])
    stat_ref[...] = jnp.concatenate([delta, lse], axis=1)
    mine = own_head(rows, width)
    pay = jnp.zeros((rows, 256), F32)
    for part, x in enumerate((q_ref[...], k_ref[...], v_ref[...], d_out)):
        pay += dot(jnp.where(mine, x, jnp.zeros_like(x)), spread(part, 256, width), 1, 0)
    pick = iota((1, HEADS), 1) == (iota((rows, 1), 0) & (GROUP - 1))
    lane = iota((rows, 128), 1)
    tail = pay[:, 128:]
    wide = jnp.zeros_like(tail)
    for base, x in ((64, lse), (67, delta)):
        own = jnp.sum(jnp.where(pick, x, 0.0), axis=1, keepdims=True)
        for n in range(3):
            piece = own.astype(BF).astype(F32)
            tail += jnp.where(lane == base + n, piece, 0.0)
            wide += jnp.where((lane & 7) == base + n - 64, piece, 0.0)
            own = own - piece
    pay = jnp.concatenate([pay[:, :128], tail], axis=1).astype(BF)
    pay_ref[...] = pay
    lane = iota((1, 128), 1)
    at = iota((4 * HEADS, 1), 0)
    low = dot(selector(64 * (at & 3) + (at >> 2), rows), pay[:, :128], 1, 0)
    at = iota((2 * HEADS, 1), 0)
    token = 64 * (at & 1) + (at >> 1)
    hi = jnp.where(lane < 64, tail, 0.0)
    high = dot(selector(token, rows), hi.astype(BF), 1, 0)
    hi = jnp.concatenate([hi[:, 64:], hi[:, :64]], axis=1)
    high += dot(selector(token + 128, rows), hi.astype(BF), 1, 0)
    wide = jnp.where(((lane >> 3) & 3) == (iota((rows, 1), 0) >> 6), wide, 0.0).astype(BF)
    picked = ((iota((1, rows), 1) & 63) == iota((2 * HEADS, 1), 0)) & (iota((2 * HEADS, 1), 0) < HEADS)
    top = jnp.concatenate([low, high, dot(picked.astype(BF), wide, 1, 0)], axis=0).astype(BF)
    for n in range(parts):
        out_ref[n, count:] = top
    each, half = width * CORES // parts, cols // CORES
    grad = dot(out, dy, 0, 0)
    for n in range(parts):
        x, c = divmod(n, CORES)
        for t in range(half // 128):
            tile = grad[each * x : each * (x + 1), half * c + 128 * t : half * c + 128 * (t + 1)]
            out_ref[n, each * t : each * (t + 1)] = tile.astype(BF)


def pack_kernel(pay_ref, out_ref):
    rows = pay_ref.shape[0]
    pay = dot(selector(packed_token(iota((rows, 1), 0)), rows), pay_ref[...], 1, 0)
    lane = iota((1, 128), 1)
    token = iota((rows, 1), 0)
    wide = stat_lanes(pay[:, 128:].astype(BF))
    wide = jnp.where((lane >> 3) == (token & 15), wide, 0.0).astype(BF)
    at, source = iota((40 * GROUP, 1), 0), iota((1, rows), 1)
    r = lax.div(at, 40)
    stats = dot(((at - 40 * r == 19 + ((source >> 4) & 1)) & (r == (source >> 5))).astype(BF), wide, 1, 0)
    for r in range(GROUP):
        low = pay[32 * r : 32 * (r + 1), :128]
        rest = pay[32 * r : 32 * (r + 1), 128:]
        pairs = jnp.concatenate([rest[:16, :64], rest[16:, :64]], axis=1)
        out_ref[r] = jnp.concatenate([low, pairs, stats[40 * r : 40 * (r + 1)]], axis=0).astype(BF)


def mid_kernel(where_ref, in_ref, pay_ref, _, out_ref):
    ring = out_ref.shape[0]
    count = in_ref.shape[1] - 8 * HEADS
    sums = jnp.sum(in_ref[:, :count].astype(F32), axis=0).astype(BF)
    each = count // 3
    few = each // ring
    at = iota((40 * ring, 1), 0)
    z = lax.div(at, 40)
    q = at - 40 * z - 22
    t = (q * 43) >> 8
    grad = dot(selector(jnp.where(q < 0, -1, each * t + few * z + q - few * t), count), sums, 1, 0)
    lane = iota((1, 128), 1)
    tops = []
    for k in range(3):
        top = in_ref[CORES * ((where_ref[0] + 1 + k) & 3) + where_ref[2], count:]
        tops += [top[:48], jnp.where((lane >> 5) == k, top[48:], jnp.zeros_like(top[48:]))]
    at, source = iota((40 * GROUP, 1), 0), iota((1, 192), 1)
    r = lax.div(at, 40)
    at = at - 40 * r
    h = (at >= 6).astype(jnp.int32)
    low = 64 * ((at - 6 * h) >> 1) + 4 * r + (at & 1) + 2 * h
    high = 64 * ((at - 12) >> 1) + 32 + 2 * r + (at & 1)
    row = jnp.where(at < 12, low, jnp.where(at < 18, high, -1))
    sel = (source == row) | ((at == 18) & ((source & 63) == 48 + r))
    top = dot(sel.astype(BF), jnp.concatenate(tops, axis=0), 1, 0)
    for r in range(GROUP):
        own = pay_ref[r].astype(F32)
        for z in range(r, ring, GROUP):
            rest = own[48:] + top[40 * r : 40 * (r + 1)] + grad[40 * z : 40 * (z + 1)]
            out_ref[z] = jnp.concatenate([own[:48], rest], axis=0).astype(BF)


def weight_end(in_ref, out_ref):
    each = out_ref.shape[0]
    parts = []
    for c in range(CORES):
        total = in_ref[c]
        for y in range(1, in_ref.shape[0] // CORES):
            total = total + in_ref[CORES * y + c]
        parts += [total[each * (t + 1) : each * (t + 2)] for t in range(3)]
    out_ref[...] = jnp.concatenate(parts, axis=1)


def window(h):
    lo = HD * h // 128 * 128
    hi = -(-HD * (h + 1) // 128) * 128
    return lo, hi


def padded(x_t, before, total):
    parts = []
    if before:
        parts.append(jnp.zeros((before, x_t.shape[1]), x_t.dtype))
    parts.append(x_t)
    after = total - before - x_t.shape[0]
    if after:
        parts.append(jnp.zeros((after, x_t.shape[1]), x_t.dtype))
    return jnp.concatenate(parts, axis=0)


def set_grads(q_win, do_win, k_pad, v_pad, q_t, k_t, do_t, lse, delta):
    scale = float(HD) ** -0.5
    probs = jnp.exp(dot(q_win, k_pad, 1, 0) * scale - lse)
    d_scores = (probs * (dot(do_win, v_pad, 1, 0) - delta)).astype(BF)
    return (
        dot(k_t, d_scores, 1, 1) * scale,
        dot(q_t, d_scores, 1, 0) * scale,
        dot(do_t, probs.astype(BF), 1, 0),
    )


def local_kernel(q_ref, k_ref, v_ref, do_ref, stat_ref, dq_ref, dk_ref, dv_ref, t_ref):
    q_t, k_t, v_t, do_t = (jnp.transpose(r[...]) for r in (q_ref, k_ref, v_ref, do_ref))
    for h in range(HEADS):
        own = slice(HD * h, HD * (h + 1))
        lo, hi = window(h)
        grads = set_grads(
            q_ref[:, lo:hi],
            do_ref[:, lo:hi],
            padded(k_t[own], HD * h - lo, hi - lo),
            padded(v_t[own], HD * h - lo, hi - lo),
            q_t[own],
            k_t[own],
            do_t[own],
            stat_ref[:, HEADS + h : HEADS + h + 1],
            stat_ref[:, h : h + 1],
        )
        for n, g in enumerate(grads):
            t_ref[n, own, :] = g
    for n, out in enumerate((dq_ref, dk_ref, dv_ref)):
        out[...] = jnp.transpose(t_ref[n])


def packed_grads(lo, hi, stat):
    scale = float(HD) ** -0.5
    one = eye(128)
    x_t = jnp.concatenate([dot(one, lo, 1, 1), dot(one, hi, 1, 1)], axis=0).astype(BF)
    q_t, k_t, v_t, do_t = (x_t[HD * n : HD * (n + 1)] for n in range(4))
    piece = iota((128, 256), 0) & 7
    lse = dot(stat, (piece < 3).astype(BF), 1, 0)
    minus = jnp.where((piece >= 3) & (piece < 6), -1.0, 0.0).astype(BF)
    probs = jnp.exp(dot(lo, padded(k_t, 0, 128), 1, 0) * scale - lse)
    d_probs = dot(jnp.concatenate([hi, stat], axis=1), jnp.concatenate([padded(v_t, 16, 128), minus], axis=0), 1, 0)
    d_scores = (probs * d_probs).astype(BF)
    return jnp.concatenate(
        [
            dot(k_t, d_scores, 1, 1) * scale,
            dot(q_t, d_scores, 1, 0) * scale,
            dot(do_t, probs.astype(BF), 1, 0),
        ],
        axis=0,
    )


def sets_kernel(where_ref, in_ref, back_ref, grad_ref):
    own = pl.ds(GROUP * where_ref[1], GROUP)
    rest = in_ref[:, 48:].astype(F32)
    grad_ref[...] = jnp.sum(rest[:, 16:], axis=0)
    blank = jnp.zeros((256, 64), F32)
    token = iota((256, 1), 0)
    mine = in_ref[own, 48:].astype(F32)[:, 16:24].reshape(8 * GROUP, 128).astype(BF)
    stat = stat_rows(mine, 8 * (token >> 5) + 3 + ((token >> 4) & 1), token & 15)
    pairs = in_ref[own, 32:48].astype(F32)
    hi = jnp.concatenate([pairs[:, :, :64], pairs[:, :, 64:]], axis=1).reshape(256, 64)
    hi = jnp.concatenate([hi, blank], axis=1)
    group = packed_grads(in_ref[own, :32].reshape(256, 128), hi.astype(BF), stat)
    n = token & 15
    h = (n >= 6).astype(jnp.int32)
    lanes = jnp.where(n < 12, 4 * ((n - 6 * h) >> 1) + (n & 1) + 2 * h, n - 12)
    stat = stat_rows(
        rest[:, 16:24].reshape(128, 128).astype(BF), 8 * (token >> 4) + 2 + (n >= 12).astype(jnp.int32), lanes
    )
    lo = jnp.concatenate([rest[:, :12], in_ref[:, :16].astype(F32)[:, :4]], axis=1).reshape(256, 128)
    first = in_ref[:, 32:48].astype(F32)[:, :4, :64]
    hi = jnp.concatenate([rest[:, 12:18, :64], rest[:, 12:18, 64:], first], axis=1).reshape(256, 64)
    hi = jnp.concatenate([hi, blank], axis=1)
    far = packed_grads(lo.astype(BF), hi.astype(BF), stat)
    far_token = iota((1, 256), 1)
    match = 128 * where_ref[1] + 16 * (token >> 5) + 12 + (token & 3)
    sel = ((far_token == match) & ((token & 31) < 4)).astype(BF)
    turn = jnp.concatenate([eye(256), sel], axis=1)
    hi, lo = split(jnp.concatenate([group, far], axis=1))
    total = dot(turn, hi, 1, 1) + dot(turn, lo, 1, 1)
    for src in range(GROUP):
        rows = total[32 * src : 32 * (src + 1)]
        back_ref[src, :32] = rows[:, :128].astype(BF)
        tail = [rows[:16, 128:144], rows[16:, 128:144], jnp.zeros((16, 96), F32)]
        back_ref[src, 32:] = jnp.concatenate(tail, axis=1).astype(BF)


def final_kernel(z_ref, dq_ref, dk_ref, dv_ref, grad_ref, oq_ref, ok_ref, ov_ref, ow_ref):
    weight_end(grad_ref, ow_ref)
    rows, width = dq_ref.shape
    token = iota((rows, 1), 0)
    perm_t = selector(32 * (token & 7) + 4 * ((token >> 3) & 7) + (token >> 6), rows)
    tail = z_ref[:, 32:].astype(F32)
    tail = jnp.concatenate([tail[:, :, :16], tail[:, :, 16:32]], axis=1).reshape(rows, 16)
    lanes = [z_ref[:, :32].reshape(rows, 128).astype(F32), tail, jnp.zeros((rows, 112), F32)]
    y = dot(perm_t, jnp.concatenate(lanes, axis=1).astype(BF), 1, 0).astype(BF)
    mine = own_head(rows, width)
    for n, (near, out) in enumerate(((dq_ref, oq_ref), (dk_ref, ok_ref), (dv_ref, ov_ref))):
        far = dot(y, (iota((256, 1), 0) - HD * n == lax.rem(iota((1, width), 1), HD)).astype(BF), 1, 0)
        out[...] = (near[...] + jnp.where(mine, far, 0.0)).astype(BF)


def call(kernel, outs, *args, scratch=(), smem=0, hbm=False, flops=0, room=32):
    vmem = pl.BlockSpec(memory_space=pltpu.VMEM)
    held = pl.BlockSpec(memory_space=pltpu.HBM) if hbm else vmem
    return pl.pallas_call(
        kernel,
        out_shape=outs,
        in_specs=[pl.BlockSpec(memory_space=pltpu.SMEM)] * smem + [held] * (len(args) - smem),
        out_specs=jax.tree.map(lambda _: vmem, outs),
        scratch_shapes=list(scratch),
        compiler_params=pltpu.CompilerParams(vmem_limit_bytes=room * 1024 * 1024),
        cost_estimate=pl.CostEstimate(flops=flops, bytes_accessed=2_000_000, transcendentals=0),
    )(*args)


def on_device(queries, keys, values, outputs, d_final, stats, w_out):
    q, k, v, o, dy, lse = (x[0] for x in (queries, keys, values, outputs, d_final, stats))
    rows, width = q.shape
    cols = dy.shape[1]
    blocks, ring = lax.axis_size("x"), lax.axis_size(("zh", "zl"))
    shape = jax.ShapeDtypeStruct

    def exchange(x, axes):
        return lax.all_to_all(x, axes, 0, 0, tiled=True)

    ins = (dy, o, w_out, lse.T, q, k, v)
    parts = blocks * CORES
    outs = (
        shape((parts, width * cols // parts // 128 + 8 * HEADS, 128), BF),
        shape((rows, width), BF),
        shape((rows, 256), BF),
        shape((rows, 2 * HEADS), F32),
    )
    out, d_out, pay, stat = call(
        front_kernel,
        outs,
        *ins,
        hbm=True,
        room=ROOM,
        scratch=[pltpu.VMEM(x.shape, x.dtype) for x in ins] + [pltpu.SemaphoreType.DMA((len(ins),))],
        flops=1_000_000_000,
    )
    where = jnp.stack([lax.axis_index(a) for a in ("x", "zh", "c")]).astype(jnp.int32)
    over_x = exchange(out, ("x", "c"))
    pay = call(pack_kernel, shape((GROUP, 88, 128), BF), pay, flops=100_000_000)
    near = call(
        local_kernel,
        (shape((rows, width), F32),) * 3,
        q, k, v, d_out, stat,
        scratch=[pltpu.VMEM((3, width, rows), F32)],
        flops=1_000_000_000,
    )
    out = call(mid_kernel, shape((ring, 88, 128), BF), where, over_x, pay, near[0], smem=1, flops=100_000_000)
    over_z = exchange(out, ("zh", "zl"))
    back, grad = call(
        sets_kernel, (shape((GROUP, 48, 128), BF), shape((24, 128), F32)), where, over_z, smem=1, flops=200_000_000
    )
    z = exchange(back, "zl")
    grad = lax.all_gather(grad, ("y", "c"), axis=0)
    d_q, d_k, d_v, grad = call(
        final_kernel,
        (shape((rows, width), BF),) * 3 + (shape((width // (blocks * ring), cols), F32),),
        z, *near, grad,
        flops=300_000_000,
    )
    return d_q[None], d_k[None], d_v[None], grad


def solution(mesh):
    dp, seq = mesh.devices.shape
    fine = jax.sharding.Mesh(
        mesh.devices.reshape(dp // CORES, CORES, seq // 16, 16 // GROUP, GROUP), ("y", "c", "x", "zh", "zl")
    )
    dp_axes, seq_axes = ("y", "c"), ("x", "zh", "zl")
    placed = P(dp_axes, seq_axes, None)
    return jax.shard_map(
        on_device,
        mesh=fine,
        in_specs=(placed,) * 6 + (P(),),
        out_specs=(placed,) * 3 + (P(seq_axes, None),),
        check_vma=False,
    )
```

```python
import functools

import jax
import jax.numpy as jnp
from jax import lax
from jax.experimental import pallas as pl
from jax.experimental.pallas import tpu as pltpu
from jax.sharding import PartitionSpec as P

HEADS = 8
HD = 48
GROUP = 8
CORES = 2
ROOM = 60
BF = jnp.bfloat16
F32 = jnp.float32


def iota(shape, dim):
    return lax.broadcasted_iota(jnp.int32, shape, dim)


def dot(a, b, ca, cb):
    return lax.dot_general(a, b, (((ca,), (cb,)), ((), ())), preferred_element_type=F32)


def split(x):
    hi = x.astype(BF)
    return hi, (x - hi.astype(F32)).astype(BF)


def eye(n):
    return (iota((n, n), 0) == iota((n, n), 1)).astype(BF)


def packed_token(p):
    return 64 * (p & 3) + 8 * ((p >> 2) & 7) + (p >> 5)


def spread(part, lanes, width):
    return (iota((1, lanes), 1) - HD * part == lax.rem(iota((width, 1), 0), HD)).astype(BF)


def own_head(rows, width):
    return lax.div(iota((1, width), 1), HD) == (iota((rows, 1), 0) & (GROUP - 1))


def selector(source, count):
    return (iota((source.shape[0], count), 1) == source).astype(BF)


def pieces(x):
    parts = []
    for _ in range(3):
        parts.append(x.astype(BF).astype(F32))
        x = x - parts[-1]
    return parts


def stat_rows(rows_of, source, group):
    x = dot(selector(source, rows_of.shape[0]), rows_of, 1, 0)
    return jnp.where((iota((1, 128), 1) >> 3) == group, x, 0.0).astype(BF)


def front_kernel(*refs):
    hbm, (out_ref, do_ref, stat_ref), vmem, sems = refs[:7], refs[7:10], refs[10:17], refs[17]
    copies = [pltpu.make_async_copy(a, b, sems.at[n]) for n, (a, b) in enumerate(zip(hbm, vmem))]
    for copy in copies:
        copy.start()
    dy_ref, o_ref, w_ref, lse_ref, q_ref, k_ref, v_ref = vmem
    rows, width = o_ref.shape
    cols = dy_ref.shape[1]
    parts = out_ref.shape[0]
    count = width * cols // parts // 128
    for copy in copies[:4]:
        copy.wait()
    out, dy = o_ref[...], dy_ref[...]
    d_out = dot(dy, w_ref[...], 1, 1).astype(BF)
    do_ref[...] = d_out
    hi, lo = split(d_out.astype(F32) * out.astype(F32))
    heads = (lax.div(iota((width, 1), 0), HD) == iota((width, 128), 1)).astype(BF)
    delta = (dot(hi, heads, 1, 0) + dot(lo, heads, 1, 0))[:, :HEADS]
    lse = jnp.transpose(lse_ref[...])
    stat_ref[...] = jnp.concatenate([delta, lse], axis=1)
    each, half = width * CORES // parts, cols // CORES
    grad = dot(out, dy, 0, 0)
    for n in range(parts):
        x, c = divmod(n, CORES)
        for t in range(half // 128):
            tile = grad[each * x : each * (x + 1), half * c + 128 * t : half * c + 128 * (t + 1)]
            out_ref[n, each * t : each * (t + 1)] = tile.astype(BF)
    for copy in copies[4:]:
        copy.wait()
    at = iota((4 * HEADS, 1), 0)
    lane = iota((1, 128), 1)
    sel = selector(64 * (at & 3) + (at >> 2), rows)
    mine = lax.div(iota((1, width), 1), HD) == (at >> 2)
    pay = jnp.zeros((4 * HEADS, 256), F32)
    for part, x in enumerate((q_ref[...], k_ref[...], v_ref[...], d_out)):
        x = jnp.where(mine, dot(sel, x, 1, 0), 0.0).astype(BF)
        pay += dot(x, spread(part, 256, width), 1, 0)
    hi = jnp.where(lane < 64, pay[:, 128:], 0.0)
    swapped = jnp.concatenate([hi[:, 64:], hi[:, :64]], axis=1)
    row = iota((2 * HEADS, 1), 0)
    row = 4 * (row >> 1) + (row & 1)
    high = dot(selector(row, 4 * HEADS), hi.astype(BF), 1, 0)
    high += dot(selector(row + 2, 4 * HEADS), swapped.astype(BF), 1, 0)
    few = dot(sel, jnp.concatenate(pieces(lse) + pieces(delta), axis=1).astype(BF), 1, 0)
    few = jnp.where((iota((1, 6 * HEADS), 1) & 7) == (at >> 2), few, 0.0).astype(BF)
    wide = dot(few, ((iota((6 * HEADS, 1), 0) >> 3) == (lane & 7)).astype(BF), 1, 0)
    wide = jnp.where(((lane >> 3) & 3) == (at & 3), wide, 0.0).astype(BF)
    picked = (iota((1, 4 * HEADS), 1) >> 2) == iota((2 * HEADS, 1), 0)
    top = jnp.concatenate([pay[:, :128], high, dot(picked.astype(BF), wide, 1, 0)], axis=0).astype(BF)
    for n in range(parts):
        out_ref[n, count:] = top


def pack_kernel(q_ref, k_ref, v_ref, do_ref, stat_ref, out_ref):
    rows, width = q_ref.shape
    order = selector(packed_token(iota((rows, 1), 0)), rows)
    mine = own_head(rows, width)
    pay = jnp.zeros((rows, 256), F32)
    for part, x in enumerate((q_ref[...], k_ref[...], v_ref[...], do_ref[...])):
        pay += dot(jnp.where(mine, x, jnp.zeros_like(x)), spread(part, 256, width), 1, 0)
    pay = dot(order, pay.astype(BF), 1, 0)
    lane = iota((1, 128), 1)
    token = iota((rows, 1), 0)
    pick = iota((1, HEADS), 1) == (token & (GROUP - 1))
    wide = jnp.zeros((rows, 128), F32)
    for base, x in ((0, stat_ref[:, HEADS:]), (3, stat_ref[:, :HEADS])):
        own = jnp.sum(jnp.where(pick, x, 0.0), axis=1, keepdims=True)
        for n, piece in enumerate(pieces(own)):
            wide += jnp.where((lane & 7) == base + n, piece, 0.0)
    wide = dot(order, wide.astype(BF), 1, 0)
    wide = jnp.where((lane >> 3) == (token & 15), wide, 0.0).astype(BF)
    at, source = iota((40 * GROUP, 1), 0), iota((1, rows), 1)
    r = lax.div(at, 40)
    stats = dot(((at - 40 * r == 19 + ((source >> 4) & 1)) & (r == (source >> 5))).astype(BF), wide, 1, 0)
    for r in range(GROUP):
        low = pay[32 * r : 32 * (r + 1), :128]
        rest = pay[32 * r : 32 * (r + 1), 128:]
        pairs = jnp.concatenate([rest[:16, :64], rest[16:, :64]], axis=1)
        out_ref[r] = jnp.concatenate([low, pairs, stats[40 * r : 40 * (r + 1)]], axis=0).astype(BF)


def mid_kernel(where_ref, in_ref, pay_ref, _, out_ref):
    ring = out_ref.shape[0]
    count = in_ref.shape[1] - 8 * HEADS
    sums = jnp.sum(in_ref[:, :count].astype(F32), axis=0).astype(BF)
    each = count // 3
    few = each // ring
    at = iota((40 * ring, 1), 0)
    z = lax.div(at, 40)
    q = at - 40 * z - 22
    t = (q * 43) >> 8
    grad = dot(selector(jnp.where(q < 0, -1, each * t + few * z + q - few * t), count), sums, 1, 0)
    lane = iota((1, 128), 1)
    tops = []
    for k in range(3):
        top = in_ref[CORES * ((where_ref[0] + 1 + k) & 3) + where_ref[2], count:]
        tops += [top[:48], jnp.where((lane >> 5) == k, top[48:], jnp.zeros_like(top[48:]))]
    at, source = iota((40 * GROUP, 1), 0), iota((1, 192), 1)
    r = lax.div(at, 40)
    at = at - 40 * r
    h = (at >= 6).astype(jnp.int32)
    low = 64 * ((at - 6 * h) >> 1) + 4 * r + (at & 1) + 2 * h
    high = 64 * ((at - 12) >> 1) + 32 + 2 * r + (at & 1)
    row = jnp.where(at < 12, low, jnp.where(at < 18, high, -1))
    sel = (source == row) | ((at == 18) & ((source & 63) == 48 + r))
    top = dot(sel.astype(BF), jnp.concatenate(tops, axis=0), 1, 0)
    for r in range(GROUP):
        own = pay_ref[r].astype(F32)
        for z in range(r, ring, GROUP):
            rest = own[48:] + top[40 * r : 40 * (r + 1)] + grad[40 * z : 40 * (z + 1)]
            out_ref[z] = jnp.concatenate([own[:48], rest], axis=0).astype(BF)


def weight_end(in_ref, out_ref):
    each = out_ref.shape[0]
    parts = []
    for c in range(CORES):
        total = in_ref[c]
        for y in range(1, in_ref.shape[0] // CORES):
            total = total + in_ref[CORES * y + c]
        parts += [total[each * (t + 1) : each * (t + 2)] for t in range(3)]
    out_ref[...] = jnp.concatenate(parts, axis=1)


def window(h):
    lo = HD * h // 128 * 128
    hi = -(-HD * (h + 1) // 128) * 128
    return lo, hi


def padded(x_t, before, total):
    parts = []
    if before:
        parts.append(jnp.zeros((before, x_t.shape[1]), x_t.dtype))
    parts.append(x_t)
    after = total - before - x_t.shape[0]
    if after:
        parts.append(jnp.zeros((after, x_t.shape[1]), x_t.dtype))
    return jnp.concatenate(parts, axis=0)


def set_grads(q_win, do_win, k_pad, v_pad, q_t, k_t, do_t, lse, delta):
    scale = float(HD) ** -0.5
    probs = jnp.exp(dot(q_win, k_pad, 1, 0) * scale - lse)
    d_scores = (probs * (dot(do_win, v_pad, 1, 0) - delta)).astype(BF)
    return (
        dot(k_t, d_scores, 1, 1) * scale,
        dot(q_t, d_scores, 1, 0) * scale,
        dot(do_t, probs.astype(BF), 1, 0),
    )


def local_kernel(q_ref, k_ref, v_ref, do_ref, stat_ref, dq_ref, dk_ref, dv_ref, t_ref):
    q_t, k_t, v_t, do_t = (jnp.transpose(r[...]) for r in (q_ref, k_ref, v_ref, do_ref))
    for h in range(HEADS):
        own = slice(HD * h, HD * (h + 1))
        lo, hi = window(h)
        grads = set_grads(
            q_ref[:, lo:hi],
            do_ref[:, lo:hi],
            padded(k_t[own], HD * h - lo, hi - lo),
            padded(v_t[own], HD * h - lo, hi - lo),
            q_t[own],
            k_t[own],
            do_t[own],
            stat_ref[:, HEADS + h : HEADS + h + 1],
            stat_ref[:, h : h + 1],
        )
        for n, g in enumerate(grads):
            t_ref[n, own, :] = g
    for n, out in enumerate((dq_ref, dk_ref, dv_ref)):
        out[...] = jnp.transpose(t_ref[n])


def packed_grads(lo, hi, stat):
    scale = float(HD) ** -0.5
    x_t = jnp.concatenate([jnp.transpose(lo), jnp.transpose(hi)], axis=0)
    q_t, k_t, v_t, do_t = (x_t[HD * n : HD * (n + 1)] for n in range(4))
    piece = iota((128, 256), 0) & 7
    lse = dot(stat, (piece < 3).astype(BF), 1, 0)
    minus = jnp.where((piece >= 3) & (piece < 6), -1.0, 0.0).astype(BF)
    probs = jnp.exp(dot(lo, padded(k_t, 0, 128), 1, 0) * scale - lse)
    d_probs = dot(jnp.concatenate([hi, stat], axis=1), jnp.concatenate([padded(v_t, 16, 128), minus], axis=0), 1, 0)
    d_scores = (probs * d_probs).astype(BF)
    return jnp.concatenate(
        [
            dot(k_t, d_scores, 1, 1) * scale,
            dot(q_t, d_scores, 1, 0) * scale,
            dot(do_t, probs.astype(BF), 1, 0),
        ],
        axis=0,
    )


def sets_kernel(where_ref, in_ref, back_ref, grad_ref):
    own = pl.ds(GROUP * where_ref[1], GROUP)
    rest = in_ref[...][:, 48:].astype(F32)
    grad_ref[...] = jnp.sum(rest[:, 16:], axis=0)
    blank = jnp.zeros((256, 64), F32)
    token = iota((256, 1), 0)
    mine = in_ref[own][:, 48:].astype(F32)[:, 16:24].reshape(8 * GROUP, 128).astype(BF)
    stat = stat_rows(mine, 8 * (token >> 5) + 3 + ((token >> 4) & 1), token & 15)
    pairs = in_ref[own, 32:48].astype(F32)
    hi = jnp.concatenate([pairs[:, :, :64], pairs[:, :, 64:]], axis=1).reshape(256, 64)
    hi = jnp.concatenate([hi, blank], axis=1)
    group = packed_grads(in_ref[own, :32].reshape(256, 128), hi.astype(BF), stat)
    n = token & 15
    h = (n >= 6).astype(jnp.int32)
    lanes = jnp.where(n < 12, 4 * ((n - 6 * h) >> 1) + (n & 1) + 2 * h, n - 12)
    stat = stat_rows(
        rest[:, 16:24].reshape(128, 128).astype(BF), 8 * (token >> 4) + 2 + (n >= 12).astype(jnp.int32), lanes
    )
    lo = jnp.concatenate([rest[:, :12], in_ref[:, :16].astype(F32)[:, :4]], axis=1).reshape(256, 128)
    first = in_ref[:, 32:48].astype(F32)[:, :4, :64]
    hi = jnp.concatenate([rest[:, 12:18, :64], rest[:, 12:18, 64:], first], axis=1).reshape(256, 64)
    hi = jnp.concatenate([hi, blank], axis=1)
    far = packed_grads(lo.astype(BF), hi.astype(BF), stat)
    far_token = iota((1, 256), 1)
    match = 128 * where_ref[1] + 16 * (token >> 5) + 12 + (token & 3)
    sel = ((far_token == match) & ((token & 31) < 4)).astype(BF)
    hi, lo = split(far)
    total = jnp.transpose(group) + dot(sel, hi, 1, 1) + dot(sel, lo, 1, 1)
    for src in range(GROUP):
        rows = total[32 * src : 32 * (src + 1)]
        back_ref[src, :32] = rows[:, :128].astype(BF)
        tail = [rows[:16, 128:144], rows[16:, 128:144], jnp.zeros((16, 96), F32)]
        back_ref[src, 32:] = jnp.concatenate(tail, axis=1).astype(BF)


def final_kernel(z_ref, dq_ref, dk_ref, dv_ref, grad_ref, oq_ref, ok_ref, ov_ref, ow_ref):
    weight_end(grad_ref, ow_ref)
    rows, width = dq_ref.shape
    token = iota((rows, 1), 0)
    perm_t = selector(32 * (token & 7) + 4 * ((token >> 3) & 7) + (token >> 6), rows)
    tail = z_ref[:, 32:].astype(F32)
    tail = jnp.concatenate([tail[:, :, :16], tail[:, :, 16:32]], axis=1).reshape(rows, 16)
    lanes = [z_ref[:, :32].reshape(rows, 128).astype(F32), tail, jnp.zeros((rows, 112), F32)]
    y = dot(perm_t, jnp.concatenate(lanes, axis=1).astype(BF), 1, 0).astype(BF)
    mine = own_head(rows, width)
    for n, (near, out) in enumerate(((dq_ref, oq_ref), (dk_ref, ok_ref), (dv_ref, ov_ref))):
        far = dot(y, (iota((256, 1), 0) - HD * n == lax.rem(iota((1, width), 1), HD)).astype(BF), 1, 0)
        out[...] = (near[...] + jnp.where(mine, far, 0.0)).astype(BF)


def call(kernel, outs, *args, scratch=(), smem=0, hbm=False, flops=0, room=32):
    vmem = pl.BlockSpec(memory_space=pltpu.VMEM)
    held = pl.BlockSpec(memory_space=pltpu.HBM) if hbm else vmem
    return pl.pallas_call(
        kernel,
        out_shape=outs,
        in_specs=[pl.BlockSpec(memory_space=pltpu.SMEM)] * smem + [held] * (len(args) - smem),
        out_specs=jax.tree.map(lambda _: vmem, outs),
        scratch_shapes=list(scratch),
        compiler_params=pltpu.CompilerParams(vmem_limit_bytes=room * 1024 * 1024),
        cost_estimate=pl.CostEstimate(flops=flops, bytes_accessed=2_000_000, transcendentals=0),
    )(*args)


def on_device(queries, keys, values, outputs, d_final, stats, w_out):
    q, k, v, o, dy, lse = (x[0] for x in (queries, keys, values, outputs, d_final, stats))
    rows, width = q.shape
    cols = dy.shape[1]
    blocks, ring = lax.axis_size("x"), lax.axis_size(("zh", "zl"))
    shape = jax.ShapeDtypeStruct

    def exchange(x, axes):
        return lax.all_to_all(x, axes, 0, 0, tiled=True)

    ins = (dy, o, w_out, lse.T, q, k, v)
    parts = blocks * CORES
    outs = (
        shape((parts, width * cols // parts // 128 + 8 * HEADS, 128), BF),
        shape((rows, width), BF),
        shape((rows, 2 * HEADS), F32),
    )
    out, d_out, stat = call(
        front_kernel,
        outs,
        *ins,
        hbm=True,
        room=ROOM,
        scratch=[pltpu.VMEM(x.shape, x.dtype) for x in ins] + [pltpu.SemaphoreType.DMA((len(ins),))],
        flops=1_000_000_000,
    )
    where = jnp.stack([lax.axis_index(a) for a in ("x", "zh", "c")]).astype(jnp.int32)
    over_x = exchange(out, ("x", "c"))
    pay = call(pack_kernel, shape((GROUP, 88, 128), BF), q, k, v, d_out, stat, flops=300_000_000)
    near = call(
        local_kernel,
        (shape((rows, width), F32),) * 3,
        q, k, v, d_out, stat,
        scratch=[pltpu.VMEM((3, width, rows), F32)],
        flops=1_000_000_000,
    )
    out = call(mid_kernel, shape((ring, 88, 128), BF), where, over_x, pay, near[0], smem=1, flops=100_000_000)
    over_z = exchange(out, ("zh", "zl"))
    back, grad = call(
        sets_kernel, (shape((GROUP, 48, 128), BF), shape((24, 128), F32)), where, over_z, smem=1, flops=200_000_000
    )
    z = exchange(back, "zl")
    grad = lax.all_gather(grad, ("y", "c"), axis=0)
    d_q, d_k, d_v, grad = call(
        final_kernel,
        (shape((rows, width), BF),) * 3 + (shape((width // (blocks * ring), cols), F32),),
        z, *near, grad,
        flops=300_000_000,
    )
    return d_q[None], d_k[None], d_v[None], grad


def solution(mesh):
    dp, seq = mesh.devices.shape
    fine = jax.sharding.Mesh(
        mesh.devices.reshape(dp // CORES, CORES, seq // 16, 16 // GROUP, GROUP), ("y", "c", "x", "zh", "zl")
    )
    dp_axes, seq_axes = ("y", "c"), ("x", "zh", "zl")
    placed = P(dp_axes, seq_axes, None)
    return jax.shard_map(
        on_device,
        mesh=fine,
        in_specs=(placed,) * 6 + (P(),),
        out_specs=(placed,) * 3 + (P(seq_axes, None),),
        check_vma=False,
    )
```

```python
import functools

import jax
import jax.numpy as jnp
from jax import lax
from jax.experimental import pallas as pl
from jax.experimental.pallas import tpu as pltpu
from jax.sharding import PartitionSpec as P

HEADS = 8
HD = 48
GROUP = 8
CORES = 2
STEP = 7
ROOM = 60
BF = jnp.bfloat16
F32 = jnp.float32


def iota(shape, dim):
    return lax.broadcasted_iota(jnp.int32, shape, dim)


def dot(a, b, ca, cb):
    return lax.dot_general(a, b, (((ca,), (cb,)), ((), ())), preferred_element_type=F32)


def split(x):
    hi = x.astype(BF)
    return hi, (x - hi.astype(F32)).astype(BF)


def eye(n):
    return (iota((n, n), 0) == iota((n, n), 1)).astype(BF)


def packed_token(p):
    return 64 * (p & 3) + 8 * ((p >> 2) & 7) + (p >> 5)


def spread(part, lanes, width):
    return (iota((1, lanes), 1) - HD * part == lax.rem(iota((width, 1), 0), HD)).astype(BF)


def own_head(rows, width):
    return lax.div(iota((1, width), 1), HD) == (iota((rows, 1), 0) & (GROUP - 1))


def selector(source, count):
    return (iota((source.shape[0], count), 1) == source).astype(BF)


def pieces(x):
    parts = []
    for _ in range(3):
        parts.append(x.astype(BF).astype(F32))
        x = x - parts[-1]
    return parts


def stat_rows(rows_of, source, group):
    x = dot(selector(source, rows_of.shape[0]), rows_of, 1, 0)
    return jnp.where((iota((1, 128), 1) >> 3) == group, x, 0.0).astype(BF)


def front_kernel(*refs):
    hbm, (out_ref, do_ref, stat_ref), vmem, sems = refs[:7], refs[7:10], refs[10:17], refs[17]
    copies = [pltpu.make_async_copy(a, b, sems.at[n]) for n, (a, b) in enumerate(zip(hbm, vmem))]
    for copy in copies:
        copy.start()
    dy_ref, o_ref, w_ref, lse_ref, q_ref, k_ref, v_ref = vmem
    rows, width = o_ref.shape
    cols = dy_ref.shape[1]
    parts = out_ref.shape[0]
    count = width * cols // parts // 128
    for copy in copies[:4]:
        copy.wait()
    out, dy = o_ref[...], dy_ref[...]
    d_out = dot(dy, w_ref[...], 1, 1).astype(BF)
    do_ref[...] = d_out
    hi, lo = split(d_out.astype(F32) * out.astype(F32))
    heads = (lax.div(iota((width, 1), 0), HD) == iota((width, 128), 1)).astype(BF)
    delta = (dot(hi, heads, 1, 0) + dot(lo, heads, 1, 0))[:, :HEADS]
    lse = jnp.transpose(lse_ref[...])
    stat_ref[...] = jnp.concatenate([delta, lse], axis=1)
    each, half = width * CORES // parts, cols // CORES
    grad = dot(out, dy, 0, 0)
    for n in range(parts):
        x, c = divmod(n, CORES)
        for t in range(half // 128):
            tile = grad[each * x : each * (x + 1), half * c + 128 * t : half * c + 128 * (t + 1)]
            out_ref[n, each * t : each * (t + 1)] = tile.astype(BF)
    for copy in copies[4:]:
        copy.wait()
    at = iota((4 * HEADS, 1), 0)
    lane = iota((1, 128), 1)
    sel = selector(64 * (at & 3) + (at >> 2), rows)
    mine = lax.div(iota((1, width), 1), HD) == (at >> 2)
    pay = jnp.zeros((4 * HEADS, 256), F32)
    for part, x in enumerate((q_ref[...], k_ref[...], v_ref[...], d_out)):
        x = jnp.where(mine, dot(sel, x, 1, 0), 0.0).astype(BF)
        pay += dot(x, spread(part, 256, width), 1, 0)
    hi = jnp.where(lane < 64, pay[:, 128:], 0.0)
    swapped = jnp.concatenate([hi[:, 64:], hi[:, :64]], axis=1)
    row = iota((2 * HEADS, 1), 0)
    row = 4 * (row >> 1) + (row & 1)
    high = dot(selector(row, 4 * HEADS), hi.astype(BF), 1, 0)
    high += dot(selector(row + 2, 4 * HEADS), swapped.astype(BF), 1, 0)
    few = dot(sel, jnp.concatenate(pieces(lse) + pieces(delta), axis=1).astype(BF), 1, 0)
    few = jnp.where((iota((1, 6 * HEADS), 1) & 7) == (at >> 2), few, 0.0).astype(BF)
    wide = dot(few, ((iota((6 * HEADS, 1), 0) >> 3) == (lane & 7)).astype(BF), 1, 0)
    wide = jnp.where(((lane >> 3) & 3) == (at & 3), wide, 0.0).astype(BF)
    picked = (iota((1, 4 * HEADS), 1) >> 2) == iota((2 * HEADS, 1), 0)
    top = jnp.concatenate([pay[:, :128], high, dot(picked.astype(BF), wide, 1, 0)], axis=0).astype(BF)
    for n in range(parts):
        out_ref[n, count:] = top


def pack_kernel(q_ref, k_ref, v_ref, do_ref, stat_ref, out_ref):
    rows, width = q_ref.shape
    order = selector(packed_token(iota((rows, 1), 0)), rows)
    mine = own_head(rows, width)
    pay = jnp.zeros((rows, 256), F32)
    for part, x in enumerate((q_ref[...], k_ref[...], v_ref[...], do_ref[...])):
        pay += dot(jnp.where(mine, x, jnp.zeros_like(x)), spread(part, 256, width), 1, 0)
    pay = dot(order, pay.astype(BF), 1, 0)
    lane = iota((1, 128), 1)
    token = iota((rows, 1), 0)
    pick = iota((1, HEADS), 1) == (token & (GROUP - 1))
    wide = jnp.zeros((rows, 128), F32)
    for base, x in ((0, stat_ref[:, HEADS:]), (3, stat_ref[:, :HEADS])):
        own = jnp.sum(jnp.where(pick, x, 0.0), axis=1, keepdims=True)
        for n, piece in enumerate(pieces(own)):
            wide += jnp.where((lane & 7) == base + n, piece, 0.0)
    wide = dot(order, wide.astype(BF), 1, 0)
    wide = jnp.where((lane >> 3) == (token & 15), wide, 0.0).astype(BF)
    at, source = iota((40 * GROUP, 1), 0), iota((1, rows), 1)
    r = lax.div(at, 40)
    stats = dot(((at - 40 * r == 19 + ((source >> 4) & 1)) & (r == (source >> 5))).astype(BF), wide, 1, 0)
    for r in range(GROUP):
        low = pay[32 * r : 32 * (r + 1), :128]
        rest = pay[32 * r : 32 * (r + 1), 128:]
        pairs = jnp.concatenate([rest[:16, :64], rest[16:, :64]], axis=1)
        out_ref[r] = jnp.concatenate([low, pairs, stats[40 * r : 40 * (r + 1)]], axis=0).astype(BF)


def mid_kernel(where_ref, in_ref, pay_ref, _, out_ref):
    ring = out_ref.shape[0]
    count = in_ref.shape[1] - 8 * HEADS
    sums = jnp.sum(in_ref[:, :count].astype(F32), axis=0).astype(BF)
    each = count // 3
    few = each // ring
    at = iota((40 * ring, 1), 0)
    z = lax.div(at, 40)
    q = at - 40 * z - 22
    t = (q * 43) >> 8
    grad = dot(selector(jnp.where(q < 0, -1, each * t + few * z + q - few * t), count), sums, 1, 0)
    lane = iota((1, 128), 1)
    tops = []
    for k in range(3):
        top = in_ref[CORES * ((where_ref[0] + 1 + k) & 3) + where_ref[2], count:]
        tops += [top[:48], jnp.where((lane >> 5) == k, top[48:], jnp.zeros_like(top[48:]))]
    at, source = iota((40 * GROUP, 1), 0), iota((1, 192), 1)
    r = lax.div(at, 40)
    at = at - 40 * r
    h = (at >= 6).astype(jnp.int32)
    low = 64 * ((at - 6 * h) >> 1) + 4 * r + (at & 1) + 2 * h
    high = 64 * ((at - 12) >> 1) + 32 + 2 * r + (at & 1)
    row = jnp.where(at < 12, low, jnp.where(at < 18, high, -1))
    sel = (source == row) | ((at == 18) & ((source & 63) == 48 + r))
    top = dot(sel.astype(BF), jnp.concatenate(tops, axis=0), 1, 0)
    for r in range(GROUP):
        own = pay_ref[r].astype(F32)
        for z in range(r, ring, GROUP):
            rest = own[48:] + top[40 * r : 40 * (r + 1)] + grad[40 * z : 40 * (z + 1)]
            out_ref[STEP * z % ring] = jnp.concatenate([own[:48], rest], axis=0).astype(BF)


def weight_end(in_ref, out_ref):
    each = out_ref.shape[0]
    parts = []
    for c in range(CORES):
        total = in_ref[c]
        for y in range(1, in_ref.shape[0] // CORES):
            total = total + in_ref[CORES * y + c]
        parts += [total[each * (t + 1) : each * (t + 2)] for t in range(3)]
    out_ref[...] = jnp.concatenate(parts, axis=1)


def window(h):
    lo = HD * h // 128 * 128
    hi = -(-HD * (h + 1) // 128) * 128
    return lo, hi


def padded(x_t, before, total):
    parts = []
    if before:
        parts.append(jnp.zeros((before, x_t.shape[1]), x_t.dtype))
    parts.append(x_t)
    after = total - before - x_t.shape[0]
    if after:
        parts.append(jnp.zeros((after, x_t.shape[1]), x_t.dtype))
    return jnp.concatenate(parts, axis=0)


def set_grads(q_win, do_win, k_pad, v_pad, q_t, k_t, do_t, lse, delta):
    scale = float(HD) ** -0.5
    probs = jnp.exp(dot(q_win, k_pad, 1, 0) * scale - lse)
    d_scores = (probs * (dot(do_win, v_pad, 1, 0) - delta)).astype(BF)
    return (
        dot(k_t, d_scores, 1, 1) * scale,
        dot(q_t, d_scores, 1, 0) * scale,
        dot(do_t, probs.astype(BF), 1, 0),
    )


def local_kernel(q_ref, k_ref, v_ref, do_ref, stat_ref, dq_ref, dk_ref, dv_ref, t_ref):
    q_t, k_t, v_t, do_t = (jnp.transpose(r[...]) for r in (q_ref, k_ref, v_ref, do_ref))
    for h in range(HEADS):
        own = slice(HD * h, HD * (h + 1))
        lo, hi = window(h)
        grads = set_grads(
            q_ref[:, lo:hi],
            do_ref[:, lo:hi],
            padded(k_t[own], HD * h - lo, hi - lo),
            padded(v_t[own], HD * h - lo, hi - lo),
            q_t[own],
            k_t[own],
            do_t[own],
            stat_ref[:, HEADS + h : HEADS + h + 1],
            stat_ref[:, h : h + 1],
        )
        for n, g in enumerate(grads):
            t_ref[n, own, :] = g
    for n, out in enumerate((dq_ref, dk_ref, dv_ref)):
        out[...] = jnp.transpose(t_ref[n])


def packed_grads(lo, hi, stat):
    scale = float(HD) ** -0.5
    x_t = jnp.concatenate([jnp.transpose(lo), jnp.transpose(hi)], axis=0)
    q_t, k_t, v_t, do_t = (x_t[HD * n : HD * (n + 1)] for n in range(4))
    piece = iota((128, 256), 0) & 7
    lse = dot(stat, (piece < 3).astype(BF), 1, 0)
    minus = jnp.where((piece >= 3) & (piece < 6), -1.0, 0.0).astype(BF)
    probs = jnp.exp(dot(lo, padded(k_t, 0, 128), 1, 0) * scale - lse)
    d_probs = dot(jnp.concatenate([hi, stat], axis=1), jnp.concatenate([padded(v_t, 16, 128), minus], axis=0), 1, 0)
    d_scores = (probs * d_probs).astype(BF)
    return jnp.concatenate(
        [
            dot(k_t, d_scores, 1, 1) * scale,
            dot(q_t, d_scores, 1, 0) * scale,
            dot(do_t, probs.astype(BF), 1, 0),
        ],
        axis=0,
    )


def sets_kernel(where_ref, in_ref, back_ref, grad_ref):
    ring = in_ref.shape[0]
    own = [in_ref[(GROUP * where_ref[1] + STEP * src) & (ring - 1)] for src in range(GROUP)]
    own = jnp.concatenate([x[None] for x in own], axis=0)
    rest = in_ref[...][:, 48:].astype(F32)
    grad_ref[...] = jnp.sum(rest[:, 16:], axis=0)
    blank = jnp.zeros((256, 64), F32)
    token = iota((256, 1), 0)
    mine = own[:, 48:].astype(F32)[:, 16:24].reshape(8 * GROUP, 128).astype(BF)
    stat = stat_rows(mine, 8 * (token >> 5) + 3 + ((token >> 4) & 1), token & 15)
    pairs = own[:, 32:48].astype(F32)
    hi = jnp.concatenate([pairs[:, :, :64], pairs[:, :, 64:]], axis=1).reshape(256, 64)
    hi = jnp.concatenate([hi, blank], axis=1)
    group = packed_grads(own[:, :32].reshape(256, 128), hi.astype(BF), stat)
    n = token & 15
    h = (n >= 6).astype(jnp.int32)
    lanes = jnp.where(n < 12, 4 * ((n - 6 * h) >> 1) + (n & 1) + 2 * h, n - 12)
    stat = stat_rows(
        rest[:, 16:24].reshape(128, 128).astype(BF), 8 * (token >> 4) + 2 + (n >= 12).astype(jnp.int32), lanes
    )
    lo = jnp.concatenate([rest[:, :12], in_ref[:, :16].astype(F32)[:, :4]], axis=1).reshape(256, 128)
    first = in_ref[:, 32:48].astype(F32)[:, :4, :64]
    hi = jnp.concatenate([rest[:, 12:18, :64], rest[:, 12:18, 64:], first], axis=1).reshape(256, 64)
    hi = jnp.concatenate([hi, blank], axis=1)
    far = packed_grads(lo.astype(BF), hi.astype(BF), stat)
    far_token = iota((1, 256), 1)
    place = (GROUP * where_ref[1] + STEP * (token >> 5)) & (ring - 1)
    match = 16 * place + 12 + (token & 3)
    sel = ((far_token == match) & ((token & 31) < 4)).astype(BF)
    hi, lo = split(far)
    total = jnp.transpose(group) + dot(sel, hi, 1, 1) + dot(sel, lo, 1, 1)
    for src in range(GROUP):
        rows = total[32 * src : 32 * (src + 1)]
        back_ref[src, :32] = rows[:, :128].astype(BF)
        tail = [rows[:16, 128:144], rows[16:, 128:144], jnp.zeros((16, 96), F32)]
        back_ref[src, 32:] = jnp.concatenate(tail, axis=1).astype(BF)


def final_kernel(z_ref, dq_ref, dk_ref, dv_ref, grad_ref, oq_ref, ok_ref, ov_ref, ow_ref):
    weight_end(grad_ref, ow_ref)
    rows, width = dq_ref.shape
    token = iota((rows, 1), 0)
    perm_t = selector(32 * (token & 7) + 4 * ((token >> 3) & 7) + (token >> 6), rows)
    tail = z_ref[:, 32:].astype(F32)
    tail = jnp.concatenate([tail[:, :, :16], tail[:, :, 16:32]], axis=1).reshape(rows, 16)
    lanes = [z_ref[:, :32].reshape(rows, 128).astype(F32), tail, jnp.zeros((rows, 112), F32)]
    y = dot(perm_t, jnp.concatenate(lanes, axis=1).astype(BF), 1, 0).astype(BF)
    mine = own_head(rows, width)
    for n, (near, out) in enumerate(((dq_ref, oq_ref), (dk_ref, ok_ref), (dv_ref, ov_ref))):
        far = dot(y, (iota((256, 1), 0) - HD * n == lax.rem(iota((1, width), 1), HD)).astype(BF), 1, 0)
        out[...] = (near[...] + jnp.where(mine, far, 0.0)).astype(BF)


def call(kernel, outs, *args, scratch=(), smem=0, hbm=False, flops=0, room=32):
    vmem = pl.BlockSpec(memory_space=pltpu.VMEM)
    held = pl.BlockSpec(memory_space=pltpu.HBM) if hbm else vmem
    return pl.pallas_call(
        kernel,
        out_shape=outs,
        in_specs=[pl.BlockSpec(memory_space=pltpu.SMEM)] * smem + [held] * (len(args) - smem),
        out_specs=jax.tree.map(lambda _: vmem, outs),
        scratch_shapes=list(scratch),
        compiler_params=pltpu.CompilerParams(vmem_limit_bytes=room * 1024 * 1024),
        cost_estimate=pl.CostEstimate(flops=flops, bytes_accessed=2_000_000, transcendentals=0),
    )(*args)


def on_device(queries, keys, values, outputs, d_final, stats, w_out):
    q, k, v, o, dy, lse = (x[0] for x in (queries, keys, values, outputs, d_final, stats))
    rows, width = q.shape
    cols = dy.shape[1]
    blocks, ring = lax.axis_size("x"), lax.axis_size("z")
    shape = jax.ShapeDtypeStruct

    def exchange(x, axes, groups=None):
        return lax.all_to_all(x, axes, 0, 0, axis_index_groups=groups, tiled=True)

    stepped = [[STEP * n % ring for n in range(ring)]]
    halves = [list(range(n, n + GROUP)) for n in range(0, ring, GROUP)]

    ins = (dy, o, w_out, lse.T, q, k, v)
    parts = blocks * CORES
    outs = (
        shape((parts, width * cols // parts // 128 + 8 * HEADS, 128), BF),
        shape((rows, width), BF),
        shape((rows, 2 * HEADS), F32),
    )
    out, d_out, stat = call(
        front_kernel,
        outs,
        *ins,
        hbm=True,
        room=ROOM,
        scratch=[pltpu.VMEM(x.shape, x.dtype) for x in ins] + [pltpu.SemaphoreType.DMA((len(ins),))],
        flops=1_000_000_000,
    )
    where = [lax.axis_index("x"), lax.axis_index("z") // GROUP, lax.axis_index("c")]
    where = jnp.stack(where).astype(jnp.int32)
    over_x = exchange(out, ("x", "c"))
    pay = call(pack_kernel, shape((GROUP, 88, 128), BF), q, k, v, d_out, stat, flops=300_000_000)
    near = call(
        local_kernel,
        (shape((rows, width), F32),) * 3,
        q, k, v, d_out, stat,
        scratch=[pltpu.VMEM((3, width, rows), F32)],
        flops=1_000_000_000,
    )
    out = call(mid_kernel, shape((ring, 88, 128), BF), where, over_x, pay, near[0], smem=1, flops=100_000_000)
    over_z = exchange(out, "z", stepped)
    back, grad = call(
        sets_kernel, (shape((GROUP, 48, 128), BF), shape((24, 128), F32)), where, over_z, smem=1, flops=200_000_000
    )
    z = exchange(back, "z", halves)
    grad = lax.all_gather(grad, ("y", "c"), axis=0)
    d_q, d_k, d_v, grad = call(
        final_kernel,
        (shape((rows, width), BF),) * 3 + (shape((width // (blocks * ring), cols), F32),),
        z, *near, grad,
        flops=300_000_000,
    )
    return d_q[None], d_k[None], d_v[None], grad


def solution(mesh):
    dp, seq = mesh.devices.shape
    fine = jax.sharding.Mesh(
        mesh.devices.reshape(dp // CORES, CORES, seq // 16, 16), ("y", "c", "x", "z")
    )
    dp_axes, seq_axes = ("y", "c"), ("x", "z")
    placed = P(dp_axes, seq_axes, None)
    return jax.shard_map(
        on_device,
        mesh=fine,
        in_specs=(placed,) * 6 + (P(),),
        out_specs=(placed,) * 3 + (P(seq_axes, None),),
        check_vma=False,
    )
```
